512 devices in a mesh: tile: 32 (over x, z_hi, core), dir: 16 (over y, z_lo).
Axes of the slice: x: 4, y: 4, z: 16 (z_hi: 4, z_lo: 4; z = z_hi * 4 + z_lo), core: 2. Of those that a mesh axis runs over, the one named last changes fastest.
Arguments:
- background_prev: float32 [64, 256, 128], P(None, 'tile'), may hold values from -6 to 6
- background_now: float32 [64, 256, 128], P(None, 'tile'), may hold values from -6 to 6
- stiffness: bfloat16 [64, 256, 128], P(None, 'tile'), may hold values from 0.039794922 to 0.19921875
- drift_terms: bfloat16 [3, 64, 256, 128], P(None, None, 'tile'), may hold values from -0.079589844 to 0.079589844
- born_prev: bfloat16 [64, 64, 256, 128], P('dir', None, 'tile'), may hold values from -6 to 6
- born_now: bfloat16 [64, 64, 256, 128], P('dir', None, 'tile'), may hold values from -6 to 6
- pieces: bfloat16 [64, 1024, 32, 128], P('dir', 'tile'), may hold values from -6 to 6
- piece_target: int32 [1024, 1], P('tile'), may hold values from 0 to 31; in each aligned block of 32 rows (0 to 31, 32 to 63, ...) at most 2 rows name the same one
- piece_block: int32 [1024], P('tile'), may hold values from 0 to 15
- wavelet: float32 [4], replicated, may hold values from -24 to 24
- source_cell: int32 [3], replicated, may hold values from 0 to 63
- receiver_z: int32 [256], replicated, may hold values from 0 to 63
- receiver_x: int32 [256], replicated, may hold values from 0 to 255
- receiver_y: int32 [256], replicated, may hold values from 0 to 127
Outputs:
- born_field: float32 [64, 64, 256, 128], P('dir', None, 'tile')
- traces: float32 [64, 4, 256], P('dir')
The draws below stay inside these ranges and needn't reach their ends.
Inputs may be any that keep to these rules, and one draw needn't show every extreme that they name: `piece_target`: in each aligned block of 32 rows (the rows of one device) no tile is named by more than 2 rows; in some blocks a tile is named by exactly 2 rows.
All inputs are finite; a program needn't handle non-finite values.
Results may differ from the reference program's by a relative error of at most 0.0005.
Values may be sent and summed in bfloat16 or wider, within the bound.
No kernel may reach another device: no remote copies, remote signals or barrier semaphores. Data moves between devices by JAX's collectives and lax.ppermute only.
A program may use at most 128 MiB of HBM per device.

```python
import math
import jax
import jax.numpy as jnp
import numpy as np
from jax import lax

NZ = 64
NY = 128
CX = 8
ITERS = 4
ZPARTS = 2
CAP = 2
REC = 256
SLOTS = 32
NX = 256
DIRS = 64
ZB = 32
ROWS = 1024
N_TILE = 32


def set_ends(drawn, key, least, largest):
    index_at = [jax.random.randint(jax.random.fold_in(key, axis), (), 0, length) for axis, length in enumerate(drawn.shape)]
    longest = drawn.shape.index(max(drawn.shape))
    beside = index_at[:longest] + [(index_at[longest] + 1) % drawn.shape[longest]] + index_at[longest + 1:]
    return drawn.at[tuple(index_at)].set(least).at[tuple(beside)].set(largest)


def level_of(rng, extent, shards, least, largest):
    def one(axis_at, blocks):
        heights = jax.random.uniform(jax.random.fold_in(jax.random.fold_in(rng, 6), axis_at), (blocks,), jnp.float32, least / len(shards), largest / len(shards))
        return jnp.repeat(jnp.exp(heights), extent[axis_at] // blocks).reshape((-1,) + (1,) * (len(extent) - axis_at - 1))

    level = one(*shards[0])
    for cut in shards[1:]:
        level = level * one(*cut)
    return level


def routed_block(rng, own, number, rows, amount, top, most, skew):
    ranking = jax.random.permutation(rng, amount)
    packed, ordinary = load_shares(amount, rows * top, most, skew, True), load_shares(amount, rows * top, most, skew, False)
    places = jnp.arange(amount)

    def named(lengths, rotation):
        used = int((lengths > 0).sum())
        fixed = max(1, used // 4)
        moved = fixed + (places - fixed + rotation * (used - fixed)) % max(1, amount - fixed)
        return jnp.zeros((amount,), jnp.int32).at[ranking[jnp.where(places < fixed, places, moved)]].set(jnp.asarray(lengths, jnp.int32))

    lengths = jnp.where(number % 4 == 0, named(packed, number // 4), named(ordinary, number - number // 4 - 1))
    mixed = jax.random.permutation(jax.random.fold_in(own, 3), amount)
    giver, taker = mixed[0:amount // 2 * 2:2], mixed[1:amount // 2 * 2:2]
    slack = jnp.minimum(lengths[giver] - 1, most - lengths[taker]) // 2
    slack = jnp.where((giver == ranking[0]) | (taker == ranking[0]) | (lengths[taker] == 0), 0, jnp.maximum(slack, 0))
    moved = jax.random.randint(jax.random.fold_in(own, 4), (amount // 2,), 0, 1 << 20) % (slack + 1)
    lengths = lengths.at[giver].add(-moved).at[taker].add(moved)
    items = jnp.searchsorted(jnp.cumsum(lengths), jnp.arange(rows * top), side="right").astype(jnp.int32)
    table = items.reshape(top, rows).T
    table = table[jax.random.permutation(jax.random.fold_in(own, 1), rows)]
    rotation = jax.random.randint(jax.random.fold_in(own, 2), (rows, 1), 0, top)
    return jnp.take_along_axis(table, (jnp.arange(top)[None, :] + rotation) % top, axis=1)


def load_shares(count, total, most, skew, full):
    loads = [(1 << 20) // math.isqrt(grade ** skew) + 1 for grade in range(1, count + 1)]
    largest = most if full else min(most, max(-(-total // count), total * loads[0] // sum(loads)))
    least = 1 if total - largest >= count - 1 else 0
    holding, rest = [largest] + [least] * (count - 1), total - largest - least * (count - 1)
    while rest > 0:
        movable = [i for i in range(1, count) if holding[i] < largest] or [i for i in range(1, count) if holding[i] < most]
        mass, budget = sum([loads[i] for i in movable]), rest
        for i in movable:
            more = min(most - holding[i], max(1, budget * loads[i] // mass), rest)
            holding[i] = holding[i] + more
            rest = rest - more
    return np.array(holding)


def scatter_about(own_key, shape, width, limit, split=(), held_as=jnp.bfloat16):
    level = level_of(own_key, shape, split, -0.22, 0.18) if split else 1.0
    drawn = jax.random.normal(own_key, shape, jnp.float32) * width * level
    return jnp.minimum(jnp.maximum(drawn, -limit), limit).astype(held_as)


def setup_inputs(seed: int = 0) -> dict:
    keys = jax.random.split(jax.random.key(seed), 15)
    background_prev = scatter_about(keys[0], (NZ, NX, NY), 1.0, 6.0, ((1, 32),), jnp.float32)
    background_now = scatter_about(keys[1], (NZ, NX, NY), 1.0, 6.0, ((1, 32),), jnp.float32)
    stiffness = jnp.clip(jnp.exp(math.log(0.19921875) - 1.61066415 * jax.random.uniform(keys[2], (NZ, NX, NY), jnp.float32) ** level_of(keys[2], (NZ, NX, NY), ((1, 32),), -0.2, 0.2)), 0.039794922, 0.19921875).astype(jnp.bfloat16)
    drift_terms = jnp.clip(jax.random.uniform(keys[3], (3, NZ, NX, NY), jnp.float32, -0.079589844, 0.079589844) * level_of(keys[3], (3, NZ, NX, NY), ((2, 32),), -0.4, 0.0), -0.079589844, 0.079589844).astype(jnp.bfloat16)
    born_prev = scatter_about(keys[4], (DIRS, NZ, NX, NY), 1.0, 6.0, ((0, 16), (2, 32)))
    born_now = scatter_about(keys[5], (DIRS, NZ, NX, NY), 1.0, 6.0, ((0, 16), (2, 32)))
    pieces = scatter_about(keys[6], (DIRS, ROWS, ZB, NY), 1.0, 6.0, ((0, 16), (1, 32)))
    piece_target_keys = jax.random.split(jax.random.fold_in(keys[7], 1), ROWS // SLOTS)
    piece_target_turns = jax.random.permutation(jax.random.fold_in(keys[7], 3), ROWS // SLOTS)
    piece_target = jax.vmap(lambda own, number: routed_block(jax.random.fold_in(keys[7], 2), own, number, SLOTS, N_TILE, 1, CAP, 2))(piece_target_keys, piece_target_turns).reshape((ROWS, 1))
    piece_block = set_ends(jax.random.randint(keys[8], (ROWS,), 0, CX * ZPARTS), jax.random.fold_in(keys[8], 1), 0, (CX * ZPARTS) - 1).astype(jnp.int32)
    wavelet = scatter_about(keys[9], (ITERS,), 4.0, 24.0, (), jnp.float32)
    source_cell = jax.random.randint(keys[10], (3,), 0, min(NZ, NX, NY)).astype(jnp.int32)
    receiver_z = set_ends(jax.random.randint(keys[11], (REC,), 0, NZ), jax.random.fold_in(keys[11], 1), 0, NZ - 1).astype(jnp.int32)
    receiver_x = set_ends(jax.random.randint(keys[12], (REC,), 0, NX), jax.random.fold_in(keys[12], 1), 0, NX - 1).astype(jnp.int32)
    receiver_y = set_ends(jax.random.randint(keys[13], (REC,), 0, NY), jax.random.fold_in(keys[13], 1), 0, NY - 1).astype(jnp.int32)
    return dict(background_prev=background_prev, background_now=background_now, stiffness=stiffness, drift_terms=drift_terms, born_prev=born_prev, born_now=born_now, pieces=pieces, piece_target=piece_target, piece_block=piece_block, wavelet=wavelet, source_cell=source_cell, receiver_z=receiver_z, receiver_x=receiver_x, receiver_y=receiver_y)


SECOND_TAPS = (-205.0 / 72.0, 8.0 / 5.0, -1.0 / 5.0, 8.0 / 315.0, -1.0 / 560.0)
FIRST_TAPS = (0.0, 4.0 / 5.0, -1.0 / 5.0, 4.0 / 105.0, -1.0 / 280.0)


def shifted(padded, interior, spatial, offset):
    starts = [4, 4, 4]
    starts[spatial] = 4 + offset
    leading = padded.ndim - 3
    window = tuple([slice(None)] * leading + [slice(starts[which], starts[which] + interior[which]) for which in range(3)])
    return padded[window]


def operate(padded, stiff_wide, drift_wide):
    interior = stiff_wide.shape
    center = shifted(padded, interior, 0, 0)
    second = 3.0 * SECOND_TAPS[0] * center
    slopes = jnp.zeros_like(center)
    for spatial in range(3):
        gradient = jnp.zeros_like(center)
        for offset in range(1, 5):
            forward = shifted(padded, interior, spatial, offset)
            backward = shifted(padded, interior, spatial, -offset)
            second = second + SECOND_TAPS[offset] * (forward + backward)
            gradient = gradient + FIRST_TAPS[offset] * (forward - backward)
        slopes = slopes + drift_wide[spatial] * gradient
    return stiff_wide * second + slopes


def reference(background_prev, background_now, stiffness, drift_terms, born_prev, born_now, pieces, piece_target, piece_block, wavelet, source_cell, receiver_z, receiver_x, receiver_y):
    stiff_wide = stiffness.astype(jnp.float32)
    drift_wide = drift_terms.astype(jnp.float32)
    depth_cells, across_cells, height_cells = background_now.shape
    source_mask = ((jnp.arange(depth_cells)[:, None, None] == source_cell[0])
                   & (jnp.arange(across_cells)[None, :, None] == source_cell[1])
                   & (jnp.arange(height_cells)[None, None, :] == source_cell[2])).astype(jnp.float32)
    previous, present = background_prev, background_now
    accelerations = []
    for step_index in range(ITERS):
        acceleration = operate(jnp.pad(present, 4), stiff_wide, drift_wide)
        accelerations.append(acceleration)
        previous, present = present, 2.0 * present - previous + acceleration + wavelet[step_index] * source_mask
    targets = piece_target[:, 0]
    columns = targets * CX + piece_block % CX
    layers = piece_block // CX
    segment_ids = (layers * across_cells + columns).astype(jnp.int32)

    def one_direction(operands):
        earlier, current, piece_rows = operands
        summed = jax.ops.segment_sum(piece_rows.astype(jnp.float32), segment_ids, num_segments=ZPARTS * across_cells)
        perturb = summed.reshape(ZPARTS, across_cells, ZB, height_cells).transpose(0, 2, 1, 3).reshape(depth_cells, across_cells, height_cells)
        earlier = earlier.astype(jnp.float32)
        current = current.astype(jnp.float32)
        samples = []
        for step_index in range(ITERS):
            following = 2.0 * current - earlier + operate(jnp.pad(current, 4), stiff_wide, drift_wide) + perturb * accelerations[step_index]
            samples.append(following[receiver_z, receiver_x, receiver_y])
            earlier, current = current, following
        return current, jnp.stack(samples)

    born_field, traces = lax.map(one_direction, (born_prev, born_now, pieces))
    return born_field, traces
```

```python
import functools

import jax
import jax.numpy as jnp
import numpy as np
from jax import lax
from jax.experimental import pallas as pl
from jax.experimental.pallas import tpu as pltpu
from jax.sharding import PartitionSpec as P

ITERS = 4
CAP = 2
F = 5

CENTRE = -14350.0
SECOND = (0.0, 8064.0, -1008.0, 128.0, -9.0)
FIRST = (0.0, 672.0, -168.0, 32.0, -3.0)

BF = jnp.bfloat16
F32 = jnp.float32
VM = pltpu.VMEM
SM = pltpu.SMEM


def vspec():
    return pl.BlockSpec(memory_space=VM)


def sspec():
    return pl.BlockSpec(memory_space=SM)


def params():
    return pltpu.CompilerParams(vmem_limit_bytes=16 * 1024 * 1024)


def tap_matrix(ny):
    both = np.zeros((ny, 2 * ny), np.float32)
    for k in range(1, 5):
        for y in range(ny):
            for at, sign in ((y + k, 1.0), (y - k, -1.0)):
                if 0 <= at < ny:
                    both[at, y] = SECOND[k]
                    both[at, ny + y] = sign * FIRST[k]
    return np.concatenate([both, both], axis=0)


def pack_kernel(target, block, pieces, packed, count, label):
    directions, rows, zb, ny = pieces.shape
    tiles = packed.shape[0]

    def clear(t, c):
        count[t] = 0
        for a in range(CAP):
            label[t * CAP + a] = 0
        return c

    lax.fori_loop(0, tiles, clear, 0)

    def place(r, c):
        t = target[r]
        a = count[t]
        count[t] = a + 1
        label[t * CAP + a] = block[r] + 1
        for k in range(directions):
            at = pl.multiple_of((a * directions + k) * zb, zb)
            packed[t, pl.ds(at, zb), :] = pieces[k, r]
        return c

    lax.fori_loop(0, rows, place, 0)
    row_at = lax.broadcasted_iota(jnp.int32, (16, ny), 0)

    def name(t, c):
        held = jnp.zeros((16, ny), jnp.int32)
        for a in range(CAP):
            held = jnp.where(row_at == a, label[t * CAP + a], held)
        packed[t, CAP * directions * zb :, :] = held.astype(F32).astype(BF)
        return c

    lax.fori_loop(0, tiles, name, 0)


def pack(pieces, target, block, tiles):
    k, rows, zb, ny = pieces.shape
    return pl.pallas_call(
        pack_kernel,
        out_shape=jax.ShapeDtypeStruct((tiles, CAP * k * zb + 16, ny), pieces.dtype),
        in_specs=[sspec(), sspec(), vspec()],
        out_specs=vspec(),
        scratch_shapes=[SM((tiles,), jnp.int32), SM((tiles * CAP,), jnp.int32)],
        compiler_params=params(),
        name="pack",
    )(target, block, pieces)


def list_kernel(rz, rx, ry, where, *outs):
    row_in, y_in, at_in, row_by, y_by, at_by, count = outs
    first, planes, depth = where[0], where[1], where[2]

    def look(i, n):
        x = rx[i] - first
        inside = (x >= 0) & (x < planes)
        beside = (x >= -4) & (x < planes + 4) & jnp.logical_not(inside)

        @pl.when(inside)
        def _():
            row_in[n[0]] = x * depth + rz[i]
            y_in[n[0]] = ry[i]
            at_in[n[0]] = i

        @pl.when(beside)
        def _():
            row_by[n[1]] = (x + 4) * depth + rz[i]
            y_by[n[1]] = ry[i]
            at_by[n[1]] = i

        return n[0] + inside.astype(jnp.int32), n[1] + beside.astype(jnp.int32)

    count[0], count[1] = lax.fori_loop(0, rz.shape[0], look, (jnp.int32(0), jnp.int32(0)))


def list_receivers(rz, rx, ry, where):
    n = rz.shape[0]
    ints = jax.ShapeDtypeStruct((n,), jnp.int32)
    return pl.pallas_call(
        list_kernel,
        out_shape=(ints,) * 6 + (jax.ShapeDtypeStruct((2,), jnp.int32),),
        in_specs=[sspec()] * 4,
        out_specs=(sspec(),) * 7,
        compiler_params=params(),
        name="receivers",
    )(rz, rx, ry, where)


def at_receivers(rec, beside, read, into, gathered):
    rows, ys, ats = rec[3:6] if beside else rec[0:3]
    count = rec[6]
    for target in into:
        target[...] = jnp.zeros(target.shape, F32)
    for g in gathered:
        g[...] = jnp.zeros(g.shape, F32)
    lane = lax.broadcasted_iota(jnp.int32, gathered[0].shape, 1)

    def one(j, c):
        row, y, at = rows[j], ys[j], ats[j]
        read(row, gathered)
        to = at % 128
        for g, target in zip(gathered, into):
            moved = pltpu.roll(g[...], (to - y + 128) % 128, 1)
            target[at // 128] = target[at // 128] + jnp.where(lane == to, moved, 0.0)
        return c

    lax.fori_loop(0, count[1] if beside else count[0], one, 0)


def apply_own(cur, f, buf, ybuf, taps, coef, emit):
    nx, depth, ny = cur.shape[1:]
    for x in range(nx):
        u = cur[f, x]
        buf[4 + x, 8 : 8 + depth] = u
        top = u.astype(BF)
        rest = (u - top.astype(F32)).astype(BF)
        ybuf[x] = jnp.dot(
            jnp.concatenate([top, rest], axis=1), taps[...], preferred_element_type=F32
        )
    rows = 32

    def part(i, c):
        x, h = i // (depth // rows), i % (depth // rows)
        z0 = pl.multiple_of(h * rows, rows)
        at = 8 + z0

        def rd(px, dz):
            return buf[px, pl.ds(at + dz, rows), :]

        u = rd(4 + x, 0)
        y = ybuf[x, pl.ds(z0, rows), :]
        second = (3.0 * CENTRE) * u + y[:, :ny]
        gx = gz = None
        for k in range(1, 5):
            p, m = rd(4 + x + k, 0), rd(4 + x - k, 0)
            second = second + SECOND[k] * (p + m)
            g = FIRST[k] * (p - m)
            gx = g if gx is None else gx + g
            p, m = rd(4 + x, k), rd(4 + x, -k)
            second = second + SECOND[k] * (p + m)
            g = FIRST[k] * (p - m)
            gz = g if gz is None else gz + g

        def cf(which):
            return coef[which, x, pl.ds(z0, rows), :]

        value = cf(0) * second + cf(1) * gz + cf(2) * gx + cf(3) * y[:, ny:]
        emit(x, z0, rows, u, value)
        return c

    lax.fori_loop(0, nx * (depth // rows), part, 0)


def clear_edges(buf, depth):
    nx = buf.shape[0] - 8
    for x in range(4):
        buf[x] = jnp.zeros(buf.shape[1:], F32)
        buf[4 + nx + x] = jnp.zeros(buf.shape[1:], F32)
    zeros = jnp.zeros((8, buf.shape[2]), F32)
    for x in range(nx):
        buf[4 + x, 0:8] = zeros
        buf[4 + x, 8 + depth : 16 + depth] = zeros


def source_term(n, wav, src, x, z0, shape):
    z = lax.broadcasted_iota(jnp.int32, shape, 0) + z0
    y = lax.broadcasted_iota(jnp.int32, shape, 1)
    at = (z == src[0]) & (y == src[2])
    amount = jnp.where(x == src[1], wav[n], 0.0)
    return jnp.where(at, amount, 0.0)


def own_part(n, wav, src, cur, prev, coef, taps, part, acc, buf, ybuf):
    depth = cur.shape[2]
    clear_edges(buf, depth)
    for f in range(F):

        def emit(x, z0, rows, u, value, f=f):
            rs = pl.ds(z0, rows)
            new = 2.0 * u - prev[f, x, rs, :] + value
            if f == 0:
                acc[x, rs, :] = value
                new = new + source_term(n, wav, src, x, z0, u.shape)
            part[f, x, rs, :] = new

        apply_own(cur, f, buf, ybuf, taps, coef, emit)


def own_kernel(n, wav, src, cur, prev, coef, taps, part, acc, buf, ybuf):
    own_part(n, wav, src, cur, prev, coef, taps, part, acc, buf, ybuf)


def own_table_kernel(
    n, wav, src, *refs
):
    rec = refs[:7]
    cur, prev, coef, taps, perturb, part, acc, table, buf, ybuf, gathered, found = refs[7:]
    own_part(n, wav, src, cur, prev, coef, taps, part, acc, buf, ybuf)
    k, nx, depth, ny = perturb.shape

    def read(row, gs):
        x, z = row // depth, pl.ds(row % depth, 1)
        gs[0][0:1, :] = coef[0, x, z, :]
        gs[0][1:2, :] = coef[2, x, z, :]
        for j in range(k):
            gs[0][2 + j : 3 + j, :] = perturb[j, x, z, :]

    at_receivers(rec, False, read, [found], [gathered])
    left = found[...].reshape(16, 128)
    for term in range(3):
        rounded = left.astype(BF)
        table[16 * term : 16 * term + 16, :] = rounded
        left = left - rounded.astype(F32)
    table[48:64, :] = jnp.zeros((16, 128), BF)


def own_trace_kernel(n, wav, src, *refs):
    rec = refs[:7]
    (cur, prev, coef, taps, perturb, table_low, table_high) = refs[7:14]
    part, acc, traces, buf, ybuf, ga, gb, ta, tb = refs[14:]
    own_part(n, wav, src, cur, prev, coef, taps, part, acc, buf, ybuf)
    k, nx, depth, ny = perturb.shape

    def read_beside(row, gs):
        x, z = row // depth - 4, pl.ds(row % depth, 1)
        near = jnp.where(x < 0, 0, nx - 4)
        for f in range(F):
            second = first = jnp.zeros((1, ny), F32)
            for q in range(4):
                p = near + q
                d = p - x
                away = jnp.abs(d)
                c2 = c1 = jnp.float32(0.0)
                for t in range(1, 5):
                    c2 = jnp.where(away == t, jnp.float32(SECOND[t]), c2)
                    c1 = jnp.where(away == t, jnp.float32(FIRST[t]), c1)
                c1 = jnp.where(d < 0, -c1, c1)
                u = cur[f, p, z, :]
                second = second + c2 * u
                first = first + c1 * u
            gs[0][f : f + 1, :] = second
            gs[1][f : f + 1, :] = first

    at_receivers(rec, True, read_beside, [ta, tb], [ga, gb])
    both = jnp.zeros((16, 128), F32)
    for table in (table_low, table_high):
        for term in range(3):
            both = both + table[16 * term : 16 * term + 16, :].astype(F32)
    shares = []
    for h in range(2):
        const = both[8 * h : 8 * h + 8]
        reach = const[0:1] * ta[h] + const[1:2] * tb[h]
        shares.append(
            jnp.concatenate(
                [reach[1 + j : 2 + j] + const[2 + j : 3 + j] * reach[0:1] for j in range(k)], axis=0
            )
        )

    def read_own(row, gs):
        x, z = row // depth, pl.ds(row % depth, 1)
        for j in range(k):
            gs[0][j : j + 1, :] = part[1 + j, x, z, :] + perturb[j, x, z, :] * acc[x, z, :]

    at_receivers(rec, False, read_own, [ta], [ga])
    for h in range(2):
        traces[h * k : h * k + k, :] = shares[h] + ta[h, 0:k, :]


def near_planes(msg, f, first, rs):
    if first and f > 0:
        base = 5 + 4 * (f - 1)
        return [msg[base + p, rs, :].astype(F32) for p in range(4)]
    base = 5 * f
    near = msg[base, rs, :].astype(F32) + msg[base + 1, rs, :].astype(F32)
    return [near] + [msg[base + 1 + p, rs, :].astype(F32) for p in range(1, 4)]


def send_plane(msg, f, p, rs, new):
    top = new.astype(BF)
    if p == 0:
        msg[5 * f, rs, :] = top
        msg[5 * f + 1, rs, :] = (new - top.astype(F32)).astype(BF)
    else:
        msg[5 * f + 1 + p, rs, :] = top


def finish_part(n, part, acc_own, low_in, high_in, coef, perturb, acc, nxt, low, high, out):
    nx, depth, ny = part.shape[1:]
    rows = 16
    last = n == ITERS - 1
    for f in range(F):

        def piece(i, c, f=f):
            z0 = pl.multiple_of(i * rows, rows)
            rs = pl.ds(z0, rows)
            below = near_planes(low_in, f, n == 0, rs)
            above = near_planes(high_in, f, n == 0, rs)
            for x in range(nx):
                lower = x < 4
                planes, d, sign = (below, x, -1.0) if lower else (above, nx - 1 - x, 1.0)
                second = first = None
                for j in range(4 - d):
                    t = d + 1 + j
                    s, g = SECOND[t] * planes[j], (sign * FIRST[t]) * planes[j]
                    second = s if second is None else second + s
                    first = g if first is None else first + g
                reach = coef[0, x, rs, :] * second + coef[2, x, rs, :] * first
                if f == 0:
                    acc[x, rs, :] = acc_own[x, rs, :] + reach
                    if last:
                        continue
                    new = part[f, x, rs, :] + reach
                else:
                    new = part[f, x, rs, :] + reach + perturb[f - 1, x, rs, :] * acc[x, rs, :]
                if last:
                    out[f - 1, pl.ds(z0 * nx + x, rows, stride=nx), :] = new
                else:
                    nxt[f, x, rs, :] = new
                    send_plane(low if lower else high, f, d, rs, new)
            return c

        lax.fori_loop(0, depth // rows, piece, 0)


def sample_new(n, rec, nxt, traces, gathered, depth, k):
    offset = (n % 2) * k

    def read(row, gs):
        for j in range(k):
            gs[0][offset + j : offset + j + 1, :] = nxt[
                j + 1, row // depth, pl.ds(row % depth, 1), :
            ]

    at_receivers(rec, False, read, [traces], [gathered])


def gather_kernel(labels, *refs):
    rec = refs[:7]
    part, acc_own, low_in, high_in, coef, incoming = refs[7:13]
    nxt, perturb, low, high, traces, acc, gathered = refs[13:]
    k, nx, depth, ny = perturb.shape
    zb = (incoming.shape[1] - 16) // (CAP * k)
    perturb[...] = jnp.zeros(perturb.shape, F32)

    def add(s, c):
        label = labels[s]
        t, a = s // CAP, s % CAP

        @pl.when(label > 0)
        def _():
            b = label - 1
            x = b % nx
            z0 = pl.multiple_of((b // nx) * zb, zb)
            for j in range(k):
                at = pl.multiple_of((a * k + j) * zb, zb)
                perturb[j, x, pl.ds(z0, zb), :] = perturb[j, x, pl.ds(z0, zb), :] + incoming[
                    t, pl.ds(at, zb), :
                ].astype(F32)

        return c

    lax.fori_loop(0, incoming.shape[0] * CAP, add, 0)
    finish_part(0, part, acc_own, low_in, high_in, coef, perturb, acc, nxt, low, high, None)
    sample_new(0, rec, nxt, traces, gathered, depth, k)


def finish_kernel(n, *refs):
    rec = refs[:7]
    part, acc_own, low_in, high_in, coef, perturb = refs[7:13]
    rest = refs[13:]
    k, nx, depth, ny = perturb.shape
    if n == ITERS - 1:
        out, acc = rest
        finish_part(
            n, part, acc_own, low_in, high_in, coef, perturb, acc, None, None, None, out
        )
        return
    if n == 1:
        table, nxt, low, high, traces, acc, gathered = rest
        low[5 * F] = table[...]
        high[5 * F] = table[...]
    else:
        nxt, low, high, traces, acc, gathered = rest
    finish_part(n, part, acc_own, low_in, high_in, coef, perturb, acc, nxt, low, high, None)
    sample_new(n, rec, nxt, traces, gathered, depth, k)


def cost(flops, moved):
    return pl.CostEstimate(flops=flops, bytes_accessed=moved, transcendentals=0)


def exchange(low, high):
    count = lax.axis_size("tile")
    forward = [(i, i + 1) for i in range(count - 1)]
    backward = [(b, a) for a, b in forward]
    return lax.ppermute(high, "tile", forward), lax.ppermute(low, "tile", backward)


def swap(value):
    count = lax.axis_size("tile")
    return lax.ppermute(value, "tile", [(i, i ^ 1) for i in range(count)])


def two_terms(plane):
    top = plane.astype(BF)
    return [top, (plane - lax.reduce_precision(plane, 8, 7)).astype(BF)]


def local(
    background_prev,
    background_now,
    stiffness,
    drift_terms,
    born_prev,
    born_now,
    pieces,
    piece_target,
    piece_block,
    wavelet,
    source_cell,
    receiver_z,
    receiver_x,
    receiver_y,
):
    tiles = lax.axis_size("tile")
    place = lax.axis_index("tile")
    k = born_now.shape[0]
    depth, nx, ny = background_now.shape
    zb = pieces.shape[2]

    packed = pack(pieces, piece_target[:, 0], piece_block, tiles)
    incoming = lax.all_to_all(packed, "tile", 0, 0, tiled=True)
    names = incoming[:, CAP * k * zb : CAP * k * zb + CAP, 0]
    labels = names.astype(jnp.int32).reshape(tiles * CAP)

    def face(planes):
        near = two_terms(background_now[:, planes[0], :])
        rows = near + [background_now[:, p, :].astype(BF) for p in planes[1:]]
        born = jnp.stack([born_now[:, :, p, :] for p in planes], axis=1)
        return jnp.concatenate([jnp.stack(rows), born.reshape(k * 4, depth, ny)])

    low_in, high_in = exchange(face((0, 1, 2, 3)), face((7, 6, 5, 4)))

    where = jnp.stack([place * nx, jnp.int32(nx), jnp.int32(depth)]).astype(jnp.int32)
    rec = list_receivers(receiver_z, receiver_x, receiver_y, where)
    src = jnp.stack([source_cell[0], source_cell[1] - place * nx, source_cell[2]])

    def planes_first(background, born):
        return jnp.concatenate(
            [
                background.transpose(1, 0, 2)[None],
                born.astype(F32).transpose(0, 2, 1, 3),
            ]
        )

    cur = planes_first(background_now, born_now)
    prev = planes_first(background_prev, born_prev)
    coef = jnp.concatenate(
        [
            (stiffness.astype(F32) * (1.0 / 5040.0))[None],
            drift_terms.astype(F32) * (1.0 / 840.0),
        ]
    ).transpose(0, 2, 1, 3)
    taps = jnp.asarray(tap_matrix(ny)).astype(BF)

    state = jax.ShapeDtypeStruct((F, nx, depth, ny), F32)
    field = jax.ShapeDtypeStruct((nx, depth, ny), F32)
    faces = jax.ShapeDtypeStruct((5 * F, depth, ny), BF)
    wider = jax.ShapeDtypeStruct((5 * F + 1, depth, ny), BF)
    traced = jax.ShapeDtypeStruct((2, 8, 128), F32)
    small = VM((8, 128), F32)
    pair = VM((2, 8, 128), F32)
    work = [VM((nx + 8, depth + 16, ny), F32), VM((nx, depth, 2 * ny), F32)]
    cells = F * nx * depth * ny

    def call(kernel, name, out_shape, scratch, scalars, arrays, flops):
        return pl.pallas_call(
            kernel,
            out_shape=out_shape,
            in_specs=[sspec()] * len(scalars) + [vspec()] * len(arrays),
            out_specs=tuple(vspec() for _ in out_shape),
            scratch_shapes=scratch,
            compiler_params=params(),
            cost_estimate=cost(flops * cells, 16 * cells),
            name=name,
        )(*scalars, *arrays)

    records = []
    perturb = table = tables = None
    for n in range(ITERS):
        name = "own%d" % (n + 1)
        start = (wavelet, src)
        arrays = (cur, prev, coef, taps)
        if n == 1:
            part, acc, table = call(
                functools.partial(own_table_kernel, n),
                name,
                (state, field, jax.ShapeDtypeStruct((64, 128), BF)),
                work + [small, pair],
                start + tuple(rec),
                arrays + (perturb,),
                80,
            )
        elif n == ITERS - 1:
            part, acc, mine = call(
                functools.partial(own_trace_kernel, n),
                name,
                (state, field, jax.ShapeDtypeStruct((8, 128), F32)),
                work + [small, small, pair, pair],
                start + tuple(rec),
                arrays + (perturb,) + tables,
                80,
            )
        else:
            part, acc = call(
                functools.partial(own_kernel, n), name, (state, field), work, start, arrays, 80
            )
        arrays = (part, acc, low_in, high_in, coef)
        name = "finish%d" % (n + 1)
        keep = VM((nx, depth, ny), F32)
        if n == 0:
            nxt, perturb, low, high, traces = call(
                gather_kernel,
                name,
                (state, jax.ShapeDtypeStruct((k, nx, depth, ny), F32), faces, faces, traced),
                [keep, small],
                (labels,) + tuple(rec),
                arrays + (incoming,),
                20,
            )
        elif n == ITERS - 1:
            (born,) = call(
                functools.partial(finish_kernel, n),
                name,
                (jax.ShapeDtypeStruct((k, depth * nx, ny), F32),),
                [keep],
                tuple(rec),
                arrays + (perturb,),
                20,
            )
            break
        else:
            face_type = wider if n == 1 else faces
            nxt, low, high, traces = call(
                functools.partial(finish_kernel, n),
                name,
                (state, face_type, face_type, traced),
                [keep, small],
                tuple(rec),
                arrays + (perturb,) + ((table,) if n == 1 else ()),
                20,
            )
        records.append(traces)
        low_in, high_in = exchange(low, high)
        if n == 1:
            tables = (low_in[5 * F], high_in[5 * F])
        prev, cur = cur, nxt

    early = jnp.stack([records[0] + records[1], records[2]])
    early = early + swap(early)
    odd = place % 2
    half = jnp.where(odd == 0, early[0], early[1])
    message = jnp.concatenate([half, mine[None]])
    message, low_in, high_in = lax.optimization_barrier((message, low_in, high_in))
    groups = [list(range(c, tiles, 2)) for c in range(2)]
    copies = lax.all_to_all(
        jnp.broadcast_to(message[None], (tiles // 2,) + message.shape),
        "tile",
        0,
        0,
        axis_index_groups=groups,
        tiled=True,
    )
    total = jnp.sum(copies, axis=0)
    other = swap(total)
    ours, theirs = total[:2], other[:2]
    first_two = jnp.where(odd == 0, ours, theirs).reshape(2, 2, k, 128)
    third = jnp.where(odd == 0, theirs, ours)[:, :k]
    fourth = (total[2] + other[2]).reshape(2, k, 128)
    steps = jnp.concatenate([first_two, third[:, None], fourth[:, None]], axis=1)
    traces = steps.transpose(2, 1, 0, 3).reshape(k, ITERS, 256)
    return born.reshape(k, depth, nx, ny), traces


def solution(mesh):
    placed = (
        P(None, "tile", None),
        P(None, "tile", None),
        P(None, "tile", None),
        P(None, None, "tile", None),
        P("dir", None, "tile", None),
        P("dir", None, "tile", None),
        P("dir", "tile", None, None),
        P("tile", None),
        P("tile"),
        P(),
        P(),
        P(),
        P(),
        P(),
    )
    return jax.shard_map(
        local,
        mesh=mesh,
        in_specs=placed,
        out_specs=(P("dir", None, "tile", None), P("dir", None, None)),
        check_vma=False,
    )
```

```python
import functools

import jax
import jax.numpy as jnp
import numpy as np
from jax import lax
from jax.experimental import pallas as pl
from jax.experimental.pallas import tpu as pltpu
from jax.sharding import PartitionSpec as P

ITERS = 4
CAP = 2
F = 5

CENTRE = -14350.0
SECOND = (0.0, 8064.0, -1008.0, 128.0, -9.0)
FIRST = (0.0, 672.0, -168.0, 32.0, -3.0)

BF = jnp.bfloat16
F32 = jnp.float32
VM = pltpu.VMEM
SM = pltpu.SMEM


def vspec():
    return pl.BlockSpec(memory_space=VM)


def sspec():
    return pl.BlockSpec(memory_space=SM)


def params(mib=16):
    return pltpu.CompilerParams(vmem_limit_bytes=mib * 1024 * 1024)


def tap_matrix(ny):
    both = np.zeros((ny, 2 * ny), np.float32)
    for k in range(1, 5):
        for y in range(ny):
            for at, sign in ((y + k, 1.0), (y - k, -1.0)):
                if 0 <= at < ny:
                    both[at, y] = SECOND[k]
                    both[at, ny + y] = sign * FIRST[k]
    return np.concatenate([both, both], axis=0)


def pack_kernel(target, block, pieces, packed, count, label):
    directions, rows, zb, ny = pieces.shape
    tiles = packed.shape[0]

    def clear(t, c):
        count[t] = 0
        for a in range(CAP):
            label[t * CAP + a] = 0
        return c

    lax.fori_loop(0, tiles, clear, 0)

    def place(r, c):
        t = target[r]
        a = count[t]
        count[t] = a + 1
        label[t * CAP + a] = block[r] + 1
        for k in range(directions):
            at = pl.multiple_of((a * directions + k) * zb, zb)
            packed[t, pl.ds(at, zb), :] = pieces[k, r]
        return c

    lax.fori_loop(0, rows, place, 0)
    lane_at = lax.broadcasted_iota(jnp.int32, (16, ny), 1)

    def name(t, c):
        held = jnp.zeros((16, ny), jnp.int32)
        for a in range(CAP):
            held = jnp.where(lane_at == a, label[t * CAP + a], held)
        packed[t, CAP * directions * zb :, :] = held.astype(F32).astype(BF)
        return c

    lax.fori_loop(0, tiles, name, 0)


def pack(pieces, target, block, tiles):
    k, rows, zb, ny = pieces.shape
    return pl.pallas_call(
        pack_kernel,
        out_shape=jax.ShapeDtypeStruct((tiles, CAP * k * zb + 16, ny), pieces.dtype),
        in_specs=[sspec(), sspec(), vspec()],
        out_specs=vspec(),
        scratch_shapes=[SM((tiles,), jnp.int32), SM((tiles * CAP,), jnp.int32)],
        compiler_params=params(),
        name="pack",
    )(target, block, pieces)


def list_kernel(rz, rx, ry, where, rec):
    first, planes, depth = where[0], where[1], where[2]

    def look(i, n):
        x = rx[i] - first
        inside = (x >= 0) & (x < planes)
        beside = (x >= -4) & (x < planes + 4) & jnp.logical_not(inside)

        @pl.when(inside)
        def _():
            rec[0, n[0]] = x * depth + rz[i]
            rec[1, n[0]] = ry[i]
            rec[2, n[0]] = i

        @pl.when(beside)
        def _():
            rec[3, n[1]] = (x + 4) * depth + rz[i]
            rec[4, n[1]] = ry[i]
            rec[5, n[1]] = i

        return n[0] + inside.astype(jnp.int32), n[1] + beside.astype(jnp.int32)

    inner, outer = lax.fori_loop(0, rz.shape[0], look, (jnp.int32(0), jnp.int32(0)))
    rec[6, 0] = inner
    rec[6, 1] = outer


def list_receivers(rz, rx, ry, where):
    n = rz.shape[0]
    return pl.pallas_call(
        list_kernel,
        out_shape=jax.ShapeDtypeStruct((8, n), jnp.int32),
        in_specs=[sspec()] * 4,
        out_specs=sspec(),
        compiler_params=params(),
        name="receivers",
    )(rz, rx, ry, where)


def at_receivers(rec, read, into, gathered):
    for target in into:
        target[...] = jnp.zeros(target.shape, F32)
    for g in gathered:
        g[...] = jnp.zeros(g.shape, F32)
    lane = lax.broadcasted_iota(jnp.int32, gathered[0].shape, 1)

    def one(j, c):
        row, y, at = rec[0, j], rec[1, j], rec[2, j]
        read(row, gathered)
        to = at % 128
        for g, target in zip(gathered, into):
            moved = pltpu.roll(g[...], (to - y + 128) % 128, 1)
            target[at // 128] = target[at // 128] + jnp.where(lane == to, moved, 0.0)
        return c

    lax.fori_loop(0, rec[6, 0], one, 0)


def apply_own(cur, f, buf, ybuf, taps, coef, emit):
    nx, depth, ny = cur.shape[1:]
    for x in range(nx):
        u = cur[f, x]
        buf[4 + x, 8 : 8 + depth] = u
        top = u.astype(BF)
        rest = (u - top.astype(F32)).astype(BF)
        ybuf[x] = jnp.dot(
            jnp.concatenate([top, rest], axis=1), taps[...], preferred_element_type=F32
        )
    rows = 32

    def part(i, c):
        x, h = i // (depth // rows), i % (depth // rows)
        z0 = pl.multiple_of(h * rows, rows)
        at = 8 + z0

        def rd(px, dz):
            return buf[px, pl.ds(at + dz, rows), :]

        u = rd(4 + x, 0)
        y = ybuf[x, pl.ds(z0, rows), :]
        second = (3.0 * CENTRE) * u + y[:, :ny]
        gx = gz = None
        for k in range(1, 5):
            p, m = rd(4 + x + k, 0), rd(4 + x - k, 0)
            second = second + SECOND[k] * (p + m)
            g = FIRST[k] * (p - m)
            gx = g if gx is None else gx + g
            p, m = rd(4 + x, k), rd(4 + x, -k)
            second = second + SECOND[k] * (p + m)
            g = FIRST[k] * (p - m)
            gz = g if gz is None else gz + g

        def cf(which):
            return coef[which, x, pl.ds(z0, rows), :]

        value = cf(0) * second + cf(1) * gz + cf(2) * gx + cf(3) * y[:, ny:]
        emit(x, z0, rows, u, value)
        return c

    lax.fori_loop(0, nx * (depth // rows), part, 0)


def clear_edges(buf, depth):
    nx = buf.shape[0] - 8
    for x in range(4):
        buf[x] = jnp.zeros(buf.shape[1:], F32)
        buf[4 + nx + x] = jnp.zeros(buf.shape[1:], F32)
    zeros = jnp.zeros((8, buf.shape[2]), F32)
    for x in range(nx):
        buf[4 + x, 0:8] = zeros
        buf[4 + x, 8 + depth : 16 + depth] = zeros


def source_term(n, wav, src, x, z0, shape):
    z = lax.broadcasted_iota(jnp.int32, shape, 0) + z0
    y = lax.broadcasted_iota(jnp.int32, shape, 1)
    at = (z == src[0]) & (y == src[2])
    amount = jnp.where(x == src[1], wav[n], 0.0)
    return jnp.where(at, amount, 0.0)


def own_part(n, wav, src, cur, prev, coef, taps, part, acc, buf, ybuf):
    depth = cur.shape[2]
    clear_edges(buf, depth)
    for f in range(F):

        def emit(x, z0, rows, u, value, f=f):
            rs = pl.ds(z0, rows)
            new = 2.0 * u - prev[f, x, rs, :] + value
            if f == 0:
                acc[x, rs, :] = value
                new = new + source_term(n, wav, src, x, z0, u.shape)
            part[f, x, rs, :] = new

        apply_own(cur, f, buf, ybuf, taps, coef, emit)


def own_kernel(n, wav, src, cur, prev, coef, taps, part, acc, buf, ybuf):
    own_part(n, wav, src, cur, prev, coef, taps, part, acc, buf, ybuf)


def own_table_kernel(
    n, wav, src, *refs
):
    rec, cur, prev, coef, taps, perturb, part, acc, table, buf, ybuf, gathered, found = refs
    own_part(n, wav, src, cur, prev, coef, taps, part, acc, buf, ybuf)
    k, nx, depth, ny = perturb.shape

    def read(row, gs):
        x, z = row // depth, pl.ds(row % depth, 1)
        gs[0][0:1, :] = coef[0, x, z, :]
        gs[0][1:2, :] = coef[2, x, z, :]
        for j in range(k):
            gs[0][2 + j : 3 + j, :] = perturb[j, x, z, :]

    at_receivers(rec, read, [found], [gathered])
    left = found[...].reshape(16, 128)
    for term in range(3):
        rounded = left.astype(BF)
        table[16 * term : 16 * term + 16, :] = rounded
        left = left - rounded.astype(F32)
    table[48:64, :] = jnp.zeros((16, 128), BF)


def share_kernel(*refs):
    rec, cur, prev, coef, perturb, table_low, table_high, traces = refs[:8]
    gathered, found = refs[8:14], refs[14:20]
    k, nx, depth, ny = perturb.shape
    lane = lax.broadcasted_iota(jnp.int32, (8, 128), 1)
    for ref in gathered + found:
        ref[...] = jnp.zeros(ref.shape, F32)

    g2, g1 = gathered[:2]
    t2, t1 = found[:2]

    def beside(i, c):
        row, y, at = rec[3, i], rec[4, i], rec[5, i]
        x, z = row // depth - 4, pl.ds(row % depth, 1)
        near = jnp.where(x < 0, 0, nx - 4)
        weights = []
        for q in range(4):
            d = near + q - x
            away = jnp.abs(d)
            c2 = c1 = jnp.float32(0.0)
            for t in range(1, 5):
                c2 = jnp.where(away == t, jnp.float32(SECOND[t]), c2)
                c1 = jnp.where(away == t, jnp.float32(FIRST[t]), c1)
            weights.append((c2, jnp.where(d < 0, -c1, c1)))
        for f in range(F):
            second = first = jnp.zeros((1, ny), F32)
            for q in range(4):
                u = cur[f, near + q, z, :]
                second = second + weights[q][0] * u
                first = first + weights[q][1] * u
            g2[f : f + 1, :] = second
            g1[f : f + 1, :] = first
        to = at % 128
        shift = (to - y + 128) % 128
        here = lane == to
        h = at // 128
        t2[h] = t2[h] + jnp.where(here, pltpu.roll(g2[...], shift, 1), 0.0)
        t1[h] = t1[h] + jnp.where(here, pltpu.roll(g1[...], shift, 1), 0.0)
        return c

    lax.fori_loop(0, rec[6, 1], beside, 0)
    both = jnp.zeros((16, 128), F32)
    for table in (table_low, table_high):
        for term in range(3):
            both = both + table[16 * term : 16 * term + 16, :].astype(F32)
    for h in range(2):
        const = both[8 * h : 8 * h + 8]
        reach = const[0:1] * t2[h] + const[1:2] * t1[h]
        for j in range(k):
            traces[h * k + j : h * k + j + 1, :] = (
                reach[1 + j : 2 + j] + const[2 + j : 3 + j] * reach[0:1]
            )

    for ref in found:
        ref[...] = jnp.zeros(ref.shape, F32)
    gs, gz, gx, gu, gp, gc = gathered
    fs, fz, fx, fy, fu, fc = found

    def inside(at, size, weight):
        return jnp.where((at >= 0) & (at < size), jnp.float32(weight), jnp.float32(0.0))

    def own(i, c):
        row, y, at = rec[0, i], rec[1, i], rec[2, i]
        x, z = row // depth, row % depth
        here_z = pl.ds(z, 1)
        reach = []
        for d in (1, 2, 3, 4, -1, -2, -3, -4):
            t = abs(d)
            sign = 1.0 if d > 0 else -1.0
            px, pz = jnp.clip(x + d, 0, nx - 1), jnp.clip(z + d, 0, depth - 1)
            reach.append(
                (
                    px,
                    inside(x + d, nx, SECOND[t]),
                    inside(x + d, nx, sign * FIRST[t]),
                    pl.ds(pz, 1),
                    inside(z + d, depth, SECOND[t]),
                    inside(z + d, depth, sign * FIRST[t]),
                )
            )
        for f in range(F):
            u = cur[f, x, here_z, :]
            second = (3.0 * CENTRE) * u
            along_x = along_z = jnp.zeros((1, ny), F32)
            for px, x2, x1, pz, z2, z1 in reach:
                v = cur[f, px, here_z, :]
                w = cur[f, x, pz, :]
                second = second + x2 * v + z2 * w
                along_x = along_x + x1 * v
                along_z = along_z + z1 * w
            gs[f : f + 1, :] = second
            gz[f : f + 1, :] = along_z
            gx[f : f + 1, :] = along_x
            gu[f : f + 1, :] = u
            gp[f : f + 1, :] = 2.0 * u - prev[f, x, here_z, :]
        for a in range(4):
            gc[a : a + 1, :] = coef[a, x, here_z, :]
        for j in range(k):
            gc[4 + j : 5 + j, :] = perturb[j, x, here_z, :]
        to = at % 128
        shift = to - y + 256
        here = lane == to
        h = at // 128

        def moved(ref, by=0):
            return pltpu.roll(ref[...], (shift - by) % 128, 1)

        second, along_y = moved(gs), jnp.zeros((8, 128), F32)
        for d in (1, 2, 3, 4, -1, -2, -3, -4):
            t = abs(d)
            v = moved(gu, d)
            second = second + inside(y + d, ny, SECOND[t]) * v
            along_y = along_y + inside(y + d, ny, FIRST[t] if d > 0 else -FIRST[t]) * v
        for ref, value in (
            (fs, second),
            (fz, moved(gz)),
            (fx, moved(gx)),
            (fy, along_y),
            (fu, moved(gp)),
            (fc, moved(gc)),
        ):
            ref[h] = ref[h] + jnp.where(here, value, 0.0)
        return c

    lax.fori_loop(0, rec[6, 0], own, 0)
    for h in range(2):
        con = fc[h]
        value = con[0:1] * fs[h] + con[1:2] * fz[h] + con[2:3] * fx[h] + con[3:4] * fy[h]
        base = fu[h] + value
        for j in range(k):
            at = slice(h * k + j, h * k + j + 1)
            traces[at, :] = (
                traces[at, :] + base[1 + j : 2 + j] + con[4 + j : 5 + j] * value[0:1]
            )


def near_planes(msg, f, first, rs):
    if first and f > 0:
        base = 5 + 4 * (f - 1)
        return [msg[base + p, rs, :].astype(F32) for p in range(4)]
    base = 5 * f
    near = msg[base, rs, :].astype(F32) + msg[base + 1, rs, :].astype(F32)
    return [near] + [msg[base + 1 + p, rs, :].astype(F32) for p in range(1, 4)]


def send_plane(msg, f, p, rs, new):
    top = new.astype(BF)
    if p == 0:
        msg[5 * f, rs, :] = top
        msg[5 * f + 1, rs, :] = (new - top.astype(F32)).astype(BF)
    else:
        msg[5 * f + 1 + p, rs, :] = top


def finish_part(n, part, acc_own, low_in, high_in, coef, perturb, acc, nxt, low, high, out):
    nx, depth, ny = part.shape[1:]
    rows = 16
    last = n == ITERS - 1
    for f in range(F):

        def piece(i, c, f=f):
            z0 = pl.multiple_of(i * rows, rows)
            rs = pl.ds(z0, rows)
            below = near_planes(low_in, f, n == 0, rs)
            above = near_planes(high_in, f, n == 0, rs)
            for x in range(nx):
                lower = x < 4
                planes, d, sign = (below, x, -1.0) if lower else (above, nx - 1 - x, 1.0)
                second = first = None
                for j in range(4 - d):
                    t = d + 1 + j
                    s, g = SECOND[t] * planes[j], (sign * FIRST[t]) * planes[j]
                    second = s if second is None else second + s
                    first = g if first is None else first + g
                reach = coef[0, x, rs, :] * second + coef[2, x, rs, :] * first
                if f == 0:
                    acc[x, rs, :] = acc_own[x, rs, :] + reach
                    if last:
                        continue
                    new = part[f, x, rs, :] + reach
                else:
                    new = part[f, x, rs, :] + reach + perturb[f - 1, x, rs, :] * acc[x, rs, :]
                if last:
                    out[f - 1, pl.ds(z0 * nx + x, rows, stride=nx), :] = new
                else:
                    nxt[f, x, rs, :] = new
                    send_plane(low if lower else high, f, d, rs, new)
            return c

        lax.fori_loop(0, depth // rows, piece, 0)


def sample_new(n, rec, nxt, traces, gathered, depth, k):
    offset = (n % 2) * k

    def read(row, gs):
        for j in range(k):
            gs[0][offset + j : offset + j + 1, :] = nxt[
                j + 1, row // depth, pl.ds(row % depth, 1), :
            ]

    at_receivers(rec, read, [traces], [gathered])


def gather_kernel(*refs):
    rec = refs[0]
    far = refs[1:7]
    nxt, perturb, low, high, traces = refs[7:12]
    near = refs[12:18]
    acc, gathered, names, labels, arrived, landed = refs[18:]
    loads = [pltpu.make_async_copy(a, b, landed.at[i]) for i, (a, b) in enumerate(zip(far, near))]
    for load in reversed(loads):
        load.start()
    part, acc_own, low_in, high_in, coef, incoming = near
    k, nx, depth, ny = perturb.shape
    loads[5].wait()
    zb = (incoming.shape[1] - 16) // (CAP * k)
    for t in range(incoming.shape[0]):
        names[t : t + 1, :] = (
            incoming[t, CAP * k * zb : CAP * k * zb + 16, :].astype(F32)[0:1].astype(jnp.int32)
        )
    copy = pltpu.make_async_copy(names, labels, arrived)
    copy.start()
    perturb[...] = jnp.zeros(perturb.shape, F32)
    copy.wait()

    def add(s, c):
        t, a = s // CAP, s % CAP
        label = labels[t, a]

        @pl.when(label > 0)
        def _():
            b = label - 1
            x = b % nx
            z0 = pl.multiple_of((b // nx) * zb, zb)
            for j in range(k):
                at = pl.multiple_of((a * k + j) * zb, zb)
                perturb[j, x, pl.ds(z0, zb), :] = perturb[j, x, pl.ds(z0, zb), :] + incoming[
                    t, pl.ds(at, zb), :
                ].astype(F32)

        return c

    lax.fori_loop(0, incoming.shape[0] * CAP, add, 0)
    for load in loads[:5]:
        load.wait()
    finish_part(0, part, acc_own, low_in, high_in, coef, perturb, acc, nxt, low, high, None)
    sample_new(0, rec, nxt, traces, gathered, depth, k)


def finish_kernel(n, *refs):
    if n == ITERS - 1:
        rec = None
    else:
        rec, refs = refs[0], refs[1:]
    part, acc_own, low_in, high_in, coef, perturb = refs[:6]
    rest = refs[6:]
    k, nx, depth, ny = perturb.shape
    if n == ITERS - 1:
        out, acc = rest
        finish_part(
            n, part, acc_own, low_in, high_in, coef, perturb, acc, None, None, None, out
        )
        return
    if n == 1:
        table, nxt, low, high, traces, acc, gathered = rest
        low[5 * F] = table[...]
        high[5 * F] = table[...]
    else:
        nxt, low, high, traces, acc, gathered = rest
    finish_part(n, part, acc_own, low_in, high_in, coef, perturb, acc, nxt, low, high, None)
    sample_new(n, rec, nxt, traces, gathered, depth, k)


def cost(flops, moved):
    return pl.CostEstimate(flops=flops, bytes_accessed=moved, transcendentals=0)


def exchange(low, high):
    count = lax.axis_size("tile")
    forward = [(i, i + 1) for i in range(count - 1)]
    backward = [(b, a) for a, b in forward]
    return lax.ppermute(high, "tile", forward), lax.ppermute(low, "tile", backward)


def swap(value):
    count = lax.axis_size("tile")
    return lax.ppermute(value, "tile", [(i, i ^ 1) for i in range(count)])


def two_terms(plane):
    top = plane.astype(BF)
    return [top, (plane - lax.reduce_precision(plane, 8, 7)).astype(BF)]


def local(
    background_prev,
    background_now,
    stiffness,
    drift_terms,
    born_prev,
    born_now,
    pieces,
    piece_target,
    piece_block,
    wavelet,
    source_cell,
    receiver_z,
    receiver_x,
    receiver_y,
):
    tiles = lax.axis_size("tile")
    place = lax.axis_index("tile")
    k = born_now.shape[0]
    depth, nx, ny = background_now.shape
    zb = pieces.shape[2]

    packed = pack(pieces, piece_target[:, 0], piece_block, tiles)
    incoming = lax.all_to_all(packed, "tile", 0, 0, tiled=True)

    def face(planes):
        near = two_terms(background_now[:, planes[0], :])
        rows = near + [background_now[:, p, :].astype(BF) for p in planes[1:]]
        born = jnp.stack([born_now[:, :, p, :] for p in planes], axis=1)
        return jnp.concatenate([jnp.stack(rows), born.reshape(k * 4, depth, ny)])

    low_in, high_in = exchange(face((0, 1, 2, 3)), face((7, 6, 5, 4)))

    where = jnp.stack([place * nx, jnp.int32(nx), jnp.int32(depth)]).astype(jnp.int32)
    rec = list_receivers(receiver_z, receiver_x, receiver_y, where)
    src = jnp.stack([source_cell[0], source_cell[1] - place * nx, source_cell[2]])

    def planes_first(background, born):
        return jnp.concatenate(
            [
                background.transpose(1, 0, 2)[None],
                born.astype(F32).transpose(0, 2, 1, 3),
            ]
        )

    cur = planes_first(background_now, born_now)
    prev = planes_first(background_prev, born_prev)
    coef = jnp.concatenate(
        [
            (stiffness.astype(F32) * (1.0 / 5040.0))[None],
            drift_terms.astype(F32) * (1.0 / 840.0),
        ]
    ).transpose(0, 2, 1, 3)
    taps = jnp.asarray(tap_matrix(ny)).astype(BF)

    state = jax.ShapeDtypeStruct((F, nx, depth, ny), F32)
    field = jax.ShapeDtypeStruct((nx, depth, ny), F32)
    faces = jax.ShapeDtypeStruct((5 * F, depth, ny), BF)
    wider = jax.ShapeDtypeStruct((5 * F + 1, depth, ny), BF)
    traced = jax.ShapeDtypeStruct((2, 8, 128), F32)
    small = VM((8, 128), F32)
    pair = VM((2, 8, 128), F32)
    work = [VM((nx + 8, depth + 16, ny), F32), VM((nx, depth, 2 * ny), F32)]
    cells = F * nx * depth * ny

    def call(kernel, name, out_shape, scratch, scalars, arrays, flops, spec=vspec(), mib=16):
        return pl.pallas_call(
            kernel,
            out_shape=out_shape,
            in_specs=[sspec()] * len(scalars) + [spec] * len(arrays),
            out_specs=tuple(vspec() for _ in out_shape),
            scratch_shapes=scratch,
            compiler_params=params(mib),
            cost_estimate=cost(flops * cells, 16 * cells),
            name=name,
        )(*scalars, *arrays)

    records = []
    perturb = table = tables = None
    for n in range(ITERS):
        name = "own%d" % (n + 1)
        start = (wavelet, src)
        arrays = (cur, prev, coef, taps)
        if n == 1:
            part, acc, table = call(
                functools.partial(own_table_kernel, n),
                name,
                (state, field, jax.ShapeDtypeStruct((64, 128), BF)),
                work + [small, pair],
                start + (rec,),
                arrays + (perturb,),
                80,
            )
        elif n == ITERS - 1:
            (mine,) = call(
                share_kernel,
                "share",
                (jax.ShapeDtypeStruct((8, 128), F32),),
                [small] * 6 + [pair] * 6,
                (rec,),
                (cur, prev, coef, perturb) + tables,
                20,
            )
            part, acc = call(
                functools.partial(own_kernel, n), name, (state, field), work, start, arrays, 80000
            )
        else:
            part, acc = call(
                functools.partial(own_kernel, n), name, (state, field), work, start, arrays, 80
            )
        arrays = (part, acc, low_in, high_in, coef)
        name = "finish%d" % (n + 1)
        keep = VM((nx, depth, ny), F32)
        if n == 0:
            nxt, perturb, low, high, traces = call(
                gather_kernel,
                name,
                (state, jax.ShapeDtypeStruct((k, nx, depth, ny), F32), faces, faces, traced),
                [VM(a.shape, a.dtype) for a in arrays + (incoming,)]
                + [
                    keep,
                    small,
                    VM((tiles, 128), jnp.int32),
                    SM((tiles, 128), jnp.int32),
                    pltpu.SemaphoreType.DMA,
                    pltpu.SemaphoreType.DMA((6,)),
                ],
                (rec,),
                arrays + (incoming,),
                20,
                pl.BlockSpec(memory_space=pltpu.HBM),
                58,
            )
        elif n == ITERS - 1:
            (born,) = call(
                functools.partial(finish_kernel, n),
                name,
                (jax.ShapeDtypeStruct((k, depth * nx, ny), F32),),
                [keep],
                (),
                arrays + (perturb,),
                20,
            )
            break
        else:
            face_type = wider if n == 1 else faces
            nxt, low, high, traces = call(
                functools.partial(finish_kernel, n),
                name,
                (state, face_type, face_type, traced),
                [keep, small],
                (rec,),
                arrays + (perturb,) + ((table,) if n == 1 else ()),
                20,
            )
        records.append(traces)
        low_in, high_in = exchange(low, high)
        if n == 1:
            tables = (low_in[5 * F], high_in[5 * F])
        prev, cur = cur, nxt

    early = jnp.stack([records[0] + records[1], records[2]])
    early = early + swap(early)
    odd = place % 2
    half = jnp.where(odd == 0, early[0], early[1])
    message = jnp.concatenate([half, mine[None]])
    groups = [list(range(c, tiles, 2)) for c in range(2)]
    copies = lax.all_to_all(
        jnp.broadcast_to(message[None], (tiles // 2,) + message.shape),
        "tile",
        0,
        0,
        axis_index_groups=groups,
        tiled=True,
    )
    copies, born = lax.optimization_barrier((copies, born))
    total = jnp.sum(copies, axis=0)
    other = swap(total)
    ours, theirs = total[:2], other[:2]
    first_two = jnp.where(odd == 0, ours, theirs).reshape(2, 2, k, 128)
    third = jnp.where(odd == 0, theirs, ours)[:, :k]
    fourth = (total[2] + other[2]).reshape(2, k, 128)
    steps = jnp.concatenate([first_two, third[:, None], fourth[:, None]], axis=1)
    traces = steps.transpose(2, 1, 0, 3).reshape(k, ITERS, 256)
    return born.reshape(k, depth, nx, ny), traces


def solution(mesh):
    placed = (
        P(None, "tile", None),
        P(None, "tile", None),
        P(None, "tile", None),
        P(None, None, "tile", None),
        P("dir", None, "tile", None),
        P("dir", None, "tile", None),
        P("dir", "tile", None, None),
        P("tile", None),
        P("tile"),
        P(),
        P(),
        P(),
        P(),
        P(),
    )
    return jax.shard_map(
        local,
        mesh=mesh,
        in_specs=placed,
        out_specs=(P("dir", None, "tile", None), P("dir", None, None)),
        check_vma=False,
    )
```

```python
import functools

import jax
import jax.numpy as jnp
import numpy as np
from jax import lax
from jax.experimental import pallas as pl
from jax.experimental.pallas import tpu as pltpu
from jax.sharding import PartitionSpec as P

ITERS = 4
CAP = 2
F = 5

CENTRE = -14350.0
SECOND = (0.0, 8064.0, -1008.0, 128.0, -9.0)
FIRST = (0.0, 672.0, -168.0, 32.0, -3.0)

BF = jnp.bfloat16
F32 = jnp.float32
VM = pltpu.VMEM
SM = pltpu.SMEM


def vspec():
    return pl.BlockSpec(memory_space=VM)


def sspec():
    return pl.BlockSpec(memory_space=SM)


def params(mib=16):
    return pltpu.CompilerParams(vmem_limit_bytes=mib * 1024 * 1024)


def tap_matrix(ny):
    both = np.zeros((ny, 2 * ny), np.float32)
    for k in range(1, 5):
        for y in range(ny):
            for at, sign in ((y + k, 1.0), (y - k, -1.0)):
                if 0 <= at < ny:
                    both[at, y] = SECOND[k]
                    both[at, ny + y] = sign * FIRST[k]
    return np.concatenate([both, both], axis=0)


def pack_kernel(target, block, pieces, packed, count, label):
    directions, rows, zb, ny = pieces.shape
    tiles = packed.shape[0]

    def clear(t, c):
        count[t] = 0
        for a in range(CAP):
            label[t * CAP + a] = 0
        return c

    lax.fori_loop(0, tiles, clear, 0)

    def place(r, c):
        t = target[r]
        a = count[t]
        count[t] = a + 1
        label[t * CAP + a] = block[r] + 1
        for k in range(directions):
            at = pl.multiple_of((a * directions + k) * zb, zb)
            packed[t, pl.ds(at, zb), :] = pieces[k, r]
        return c

    lax.fori_loop(0, rows, place, 0)
    lane_at = lax.broadcasted_iota(jnp.int32, (16, ny), 1)

    def name(t, c):
        held = jnp.zeros((16, ny), jnp.int32)
        for a in range(CAP):
            held = jnp.where(lane_at == a, label[t * CAP + a], held)
        packed[t, CAP * directions * zb :, :] = held.astype(F32).astype(BF)
        return c

    lax.fori_loop(0, tiles, name, 0)


def pack(pieces, target, block, tiles):
    k, rows, zb, ny = pieces.shape
    return pl.pallas_call(
        pack_kernel,
        out_shape=jax.ShapeDtypeStruct((tiles, CAP * k * zb + 16, ny), pieces.dtype),
        in_specs=[sspec(), sspec(), vspec()],
        out_specs=vspec(),
        scratch_shapes=[SM((tiles,), jnp.int32), SM((tiles * CAP,), jnp.int32)],
        compiler_params=params(),
        name="pack",
    )(target, block, pieces)


def list_kernel(rz, rx, ry, where, rec):
    first, planes, depth = where[0], where[1], where[2]

    def look(i, n):
        x = rx[i] - first
        inside = (x >= 0) & (x < planes)
        beside = (x >= -4) & (x < planes + 4) & jnp.logical_not(inside)

        @pl.when(inside)
        def _():
            rec[0, n[0]] = x * depth + rz[i]
            rec[1, n[0]] = ry[i]
            rec[2, n[0]] = i

        @pl.when(beside)
        def _():
            rec[3, n[1]] = (x + 4) * depth + rz[i]
            rec[4, n[1]] = ry[i]
            rec[5, n[1]] = i

        return n[0] + inside.astype(jnp.int32), n[1] + beside.astype(jnp.int32)

    inner, outer = lax.fori_loop(0, rz.shape[0], look, (jnp.int32(0), jnp.int32(0)))
    rec[6, 0] = inner
    rec[6, 1] = outer


def list_receivers(rz, rx, ry, where):
    n = rz.shape[0]
    return pl.pallas_call(
        list_kernel,
        out_shape=jax.ShapeDtypeStruct((8, n), jnp.int32),
        in_specs=[sspec()] * 4,
        out_specs=sspec(),
        compiler_params=params(),
        name="receivers",
    )(rz, rx, ry, where)


def at_receivers(rec, read, into, gathered):
    for target in into:
        target[...] = jnp.zeros(target.shape, F32)
    for g in gathered:
        g[...] = jnp.zeros(g.shape, F32)
    lane = lax.broadcasted_iota(jnp.int32, gathered[0].shape, 1)

    def one(j, c):
        row, y, at = rec[0, j], rec[1, j], rec[2, j]
        read(row, gathered)
        to = at % 128
        for g, target in zip(gathered, into):
            moved = pltpu.roll(g[...], (to - y + 128) % 128, 1)
            target[at // 128] = target[at // 128] + jnp.where(lane == to, moved, 0.0)
        return c

    lax.fori_loop(0, rec[6, 0], one, 0)


def apply_own(cur, f, buf, ybuf, taps, coef, emit):
    nx, depth, ny = cur.shape[1:]
    for x in range(nx):
        u = cur[f, x]
        buf[4 + x, 8 : 8 + depth] = u
        top = u.astype(BF)
        rest = (u - top.astype(F32)).astype(BF)
        ybuf[x] = jnp.dot(
            jnp.concatenate([top, rest], axis=1), taps[...], preferred_element_type=F32
        )
    rows = 32

    def part(i, c):
        x, h = i // (depth // rows), i % (depth // rows)
        z0 = pl.multiple_of(h * rows, rows)
        at = 8 + z0

        def rd(px, dz):
            return buf[px, pl.ds(at + dz, rows), :]

        u = rd(4 + x, 0)
        y = ybuf[x, pl.ds(z0, rows), :]
        second = (3.0 * CENTRE) * u + y[:, :ny]
        gx = gz = None
        for k in range(1, 5):
            p, m = rd(4 + x + k, 0), rd(4 + x - k, 0)
            second = second + SECOND[k] * (p + m)
            g = FIRST[k] * (p - m)
            gx = g if gx is None else gx + g
            p, m = rd(4 + x, k), rd(4 + x, -k)
            second = second + SECOND[k] * (p + m)
            g = FIRST[k] * (p - m)
            gz = g if gz is None else gz + g

        def cf(which):
            return coef[which, x, pl.ds(z0, rows), :]

        value = cf(0) * second + cf(1) * gz + cf(2) * gx + cf(3) * y[:, ny:]
        emit(x, z0, rows, u, value)
        return c

    lax.fori_loop(0, nx * (depth // rows), part, 0)


def clear_edges(buf, depth):
    nx = buf.shape[0] - 8
    for x in range(4):
        buf[x] = jnp.zeros(buf.shape[1:], F32)
        buf[4 + nx + x] = jnp.zeros(buf.shape[1:], F32)
    zeros = jnp.zeros((8, buf.shape[2]), F32)
    for x in range(nx):
        buf[4 + x, 0:8] = zeros
        buf[4 + x, 8 + depth : 16 + depth] = zeros


def source_term(n, wav, src, x, z0, shape):
    z = lax.broadcasted_iota(jnp.int32, shape, 0) + z0
    y = lax.broadcasted_iota(jnp.int32, shape, 1)
    at = (z == src[0]) & (y == src[2])
    amount = jnp.where(x == src[1], wav[n], 0.0)
    return jnp.where(at, amount, 0.0)


def own_part(n, wav, src, cur, prev, coef, taps, part, acc, buf, ybuf):
    depth = cur.shape[2]
    clear_edges(buf, depth)
    for f in range(F):

        def emit(x, z0, rows, u, value, f=f):
            rs = pl.ds(z0, rows)
            new = 2.0 * u - prev[f, x, rs, :] + value
            if f == 0:
                acc[x, rs, :] = value
                new = new + source_term(n, wav, src, x, z0, u.shape)
            part[f, x, rs, :] = new

        apply_own(cur, f, buf, ybuf, taps, coef, emit)


def own_kernel(n, wav, src, cur, prev, coef, taps, part, acc, buf, ybuf):
    own_part(n, wav, src, cur, prev, coef, taps, part, acc, buf, ybuf)


def own_table_kernel(
    n, wav, src, *refs
):
    rec, cur, prev, coef, taps, perturb, part, acc, table, buf, ybuf, gathered, found = refs
    own_part(n, wav, src, cur, prev, coef, taps, part, acc, buf, ybuf)
    k, nx, depth, ny = perturb.shape

    def read(row, gs):
        x, z = row // depth, pl.ds(row % depth, 1)
        gs[0][0:1, :] = coef[0, x, z, :]
        gs[0][1:2, :] = coef[2, x, z, :]
        for j in range(k):
            gs[0][2 + j : 3 + j, :] = perturb[j, x, z, :]

    at_receivers(rec, read, [found], [gathered])
    left = found[...].reshape(16, 128)
    for term in range(3):
        rounded = left.astype(BF)
        table[16 * term : 16 * term + 16, :] = rounded
        left = left - rounded.astype(F32)
    table[48:64, :] = jnp.zeros((16, 128), BF)


def share_kernel(*refs):
    rec, cur, prev, coef, perturb, table, traces = refs[:7]
    gathered, found = refs[7:13], refs[13:19]
    k, nx, depth, ny = perturb.shape
    lane = lax.broadcasted_iota(jnp.int32, (8, 128), 1)
    for ref in gathered + found:
        ref[...] = jnp.zeros(ref.shape, F32)

    g2, g1 = gathered[:2]
    t2, t1 = found[:2]

    def beside(i, c):
        row, y, at = rec[3, i], rec[4, i], rec[5, i]
        x, z = row // depth - 4, pl.ds(row % depth, 1)
        near = jnp.where(x < 0, 0, nx - 4)
        weights = []
        for q in range(4):
            d = near + q - x
            away = jnp.abs(d)
            c2 = c1 = jnp.float32(0.0)
            for t in range(1, 5):
                c2 = jnp.where(away == t, jnp.float32(SECOND[t]), c2)
                c1 = jnp.where(away == t, jnp.float32(FIRST[t]), c1)
            weights.append((c2, jnp.where(d < 0, -c1, c1)))
        for f in range(F):
            second = first = jnp.zeros((1, ny), F32)
            for q in range(4):
                u = cur[f, near + q, z, :]
                second = second + weights[q][0] * u
                first = first + weights[q][1] * u
            g2[f : f + 1, :] = second
            g1[f : f + 1, :] = first
        to = at % 128
        shift = (to - y + 128) % 128
        here = lane == to
        h = at // 128
        t2[h] = t2[h] + jnp.where(here, pltpu.roll(g2[...], shift, 1), 0.0)
        t1[h] = t1[h] + jnp.where(here, pltpu.roll(g1[...], shift, 1), 0.0)
        return c

    lax.fori_loop(0, rec[6, 1], beside, 0)
    for h in range(2):
        const = table[8 * h : 8 * h + 8, :]
        reach = const[0:1] * t2[h] + const[1:2] * t1[h]
        for j in range(k):
            traces[h * k + j : h * k + j + 1, :] = (
                reach[1 + j : 2 + j] + const[2 + j : 3 + j] * reach[0:1]
            )

    for ref in found:
        ref[...] = jnp.zeros(ref.shape, F32)
    gs, gz, gx, gu, gp, gc = gathered
    fs, fz, fx, fy, fu, fc = found

    def inside(at, size, weight):
        return jnp.where((at >= 0) & (at < size), jnp.float32(weight), jnp.float32(0.0))

    def own(i, c):
        row, y, at = rec[0, i], rec[1, i], rec[2, i]
        x, z = row // depth, row % depth
        here_z = pl.ds(z, 1)
        reach = []
        for d in (1, 2, 3, 4, -1, -2, -3, -4):
            t = abs(d)
            sign = 1.0 if d > 0 else -1.0
            px, pz = jnp.clip(x + d, 0, nx - 1), jnp.clip(z + d, 0, depth - 1)
            reach.append(
                (
                    px,
                    inside(x + d, nx, SECOND[t]),
                    inside(x + d, nx, sign * FIRST[t]),
                    pl.ds(pz, 1),
                    inside(z + d, depth, SECOND[t]),
                    inside(z + d, depth, sign * FIRST[t]),
                )
            )
        for f in range(F):
            u = cur[f, x, here_z, :]
            second = (3.0 * CENTRE) * u
            along_x = along_z = jnp.zeros((1, ny), F32)
            for px, x2, x1, pz, z2, z1 in reach:
                v = cur[f, px, here_z, :]
                w = cur[f, x, pz, :]
                second = second + x2 * v + z2 * w
                along_x = along_x + x1 * v
                along_z = along_z + z1 * w
            gs[f : f + 1, :] = second
            gz[f : f + 1, :] = along_z
            gx[f : f + 1, :] = along_x
            gu[f : f + 1, :] = u
            gp[f : f + 1, :] = 2.0 * u - prev[f, x, here_z, :]
        for a in range(4):
            gc[a : a + 1, :] = coef[a, x, here_z, :]
        for j in range(k):
            gc[4 + j : 5 + j, :] = perturb[j, x, here_z, :]
        to = at % 128
        shift = to - y + 256
        here = lane == to
        h = at // 128

        def moved(ref, by=0):
            return pltpu.roll(ref[...], (shift - by) % 128, 1)

        second, along_y = moved(gs), jnp.zeros((8, 128), F32)
        for d in (1, 2, 3, 4, -1, -2, -3, -4):
            t = abs(d)
            v = moved(gu, d)
            second = second + inside(y + d, ny, SECOND[t]) * v
            along_y = along_y + inside(y + d, ny, FIRST[t] if d > 0 else -FIRST[t]) * v
        for ref, value in (
            (fs, second),
            (fz, moved(gz)),
            (fx, moved(gx)),
            (fy, along_y),
            (fu, moved(gp)),
            (fc, moved(gc)),
        ):
            ref[h] = ref[h] + jnp.where(here, value, 0.0)
        return c

    lax.fori_loop(0, rec[6, 0], own, 0)
    for h in range(2):
        con = fc[h]
        value = con[0:1] * fs[h] + con[1:2] * fz[h] + con[2:3] * fx[h] + con[3:4] * fy[h]
        base = fu[h] + value
        for j in range(k):
            at = slice(h * k + j, h * k + j + 1)
            traces[at, :] = (
                traces[at, :] + base[1 + j : 2 + j] + con[4 + j : 5 + j] * value[0:1]
            )


def near_planes(msg, f, first, rs):
    if first and f > 0:
        base = 5 + 4 * (f - 1)
        return [msg[base + p, rs, :].astype(F32) for p in range(4)]
    base = 5 * f
    near = msg[base, rs, :].astype(F32) + msg[base + 1, rs, :].astype(F32)
    return [near] + [msg[base + 1 + p, rs, :].astype(F32) for p in range(1, 4)]


def send_plane(msg, f, p, rs, new):
    top = new.astype(BF)
    if p == 0:
        msg[5 * f, rs, :] = top
        msg[5 * f + 1, rs, :] = (new - top.astype(F32)).astype(BF)
    else:
        msg[5 * f + 1 + p, rs, :] = top


def finish_part(n, part, acc_own, low_in, high_in, coef, perturb, acc, nxt, low, high, out):
    nx, depth, ny = part.shape[1:]
    rows = 16
    last = n == ITERS - 1
    for f in range(F):

        def piece(i, c, f=f):
            z0 = pl.multiple_of(i * rows, rows)
            rs = pl.ds(z0, rows)
            below = near_planes(low_in, f, n == 0, rs)
            above = near_planes(high_in, f, n == 0, rs)
            for x in range(nx):
                lower = x < 4
                planes, d, sign = (below, x, -1.0) if lower else (above, nx - 1 - x, 1.0)
                second = first = None
                for j in range(4 - d):
                    t = d + 1 + j
                    s, g = SECOND[t] * planes[j], (sign * FIRST[t]) * planes[j]
                    second = s if second is None else second + s
                    first = g if first is None else first + g
                reach = coef[0, x, rs, :] * second + coef[2, x, rs, :] * first
                if f == 0:
                    acc[x, rs, :] = acc_own[x, rs, :] + reach
                    if last:
                        continue
                    new = part[f, x, rs, :] + reach
                else:
                    new = part[f, x, rs, :] + reach + perturb[f - 1, x, rs, :] * acc[x, rs, :]
                if last:
                    out[f - 1, pl.ds(z0 * nx + x, rows, stride=nx), :] = new
                else:
                    nxt[f, x, rs, :] = new
                    send_plane(low if lower else high, f, d, rs, new)
            return c

        lax.fori_loop(0, depth // rows, piece, 0)


def by_parity(odd, run):
    @pl.when(odd == 0)
    def _():
        run(True)

    @pl.when(odd == 1)
    def _():
        run(False)


def sample_new(n, rec, nxt, traces, gathered, depth, k):
    offset = (n % 2) * k

    def read(row, gs):
        for j in range(k):
            gs[0][offset + j : offset + j + 1, :] = nxt[
                j + 1, row // depth, pl.ds(row % depth, 1), :
            ]

    at_receivers(rec, read, [traces], [gathered])


def gather_kernel(*refs):
    src, rec = refs[:2]
    far = refs[2:8]
    nxt, perturb, away, beside, traces = refs[8:13]
    near = refs[13:19]
    acc, gathered, names, labels, arrived, landed = refs[19:]
    loads = [pltpu.make_async_copy(a, b, landed.at[i]) for i, (a, b) in enumerate(zip(far, near))]
    for load in reversed(loads):
        load.start()
    part, acc_own, away_in, beside_in, coef, incoming = near
    k, nx, depth, ny = perturb.shape
    loads[5].wait()
    zb = (incoming.shape[1] - 16) // (CAP * k)
    for t in range(incoming.shape[0]):
        names[t : t + 1, :] = (
            incoming[t, CAP * k * zb : CAP * k * zb + 16, :].astype(F32)[0:1].astype(jnp.int32)
        )
    copy = pltpu.make_async_copy(names, labels, arrived)
    copy.start()
    perturb[...] = jnp.zeros(perturb.shape, F32)
    copy.wait()

    def add(s, c):
        t, a = s // CAP, s % CAP
        label = labels[t, a]

        @pl.when(label > 0)
        def _():
            b = label - 1
            x = b % nx
            z0 = pl.multiple_of((b // nx) * zb, zb)
            for j in range(k):
                at = pl.multiple_of((a * k + j) * zb, zb)
                perturb[j, x, pl.ds(z0, zb), :] = perturb[j, x, pl.ds(z0, zb), :] + incoming[
                    t, pl.ds(at, zb), :
                ].astype(F32)

        return c

    lax.fori_loop(0, incoming.shape[0] * CAP, add, 0)
    for load in loads[:5]:
        load.wait()

    def run(even):
        low_in, high_in = (away_in, beside_in) if even else (beside_in, away_in)
        low, high = (away, beside) if even else (beside, away)
        finish_part(0, part, acc_own, low_in, high_in, coef, perturb, acc, nxt, low, high, None)

    by_parity(src[3], run)
    sample_new(0, rec, nxt, traces, gathered, depth, k)


def finish_kernel(n, src, *refs):
    last = n == ITERS - 1
    rec = None
    if not last:
        rec, refs = refs[0], refs[1:]
    part, acc_own, away_in, beside_in, coef, perturb = refs[:6]
    rest = refs[6:]
    k, nx, depth, ny = perturb.shape
    out = nxt = away = beside = None
    if last:
        out, acc = rest
    elif n == 1:
        table, nxt, away, beside, traces, acc, gathered = rest
        away[5 * F] = table[...]
        beside[5 * F] = table[...]
    else:
        nxt, away, beside, traces, found, acc, gathered = rest
        both = jnp.zeros((16, 128), F32)
        for msg in (away_in, beside_in):
            for term in range(3):
                both = both + msg[5 * F, 16 * term : 16 * term + 16, :].astype(F32)
        found[...] = both

    def run(even):
        low_in, high_in = (away_in, beside_in) if even else (beside_in, away_in)
        low, high = (away, beside) if even else (beside, away)
        finish_part(n, part, acc_own, low_in, high_in, coef, perturb, acc, nxt, low, high, out)

    by_parity(src[3], run)
    if not last:
        sample_new(n, rec, nxt, traces, gathered, depth, k)


def cost(flops, moved):
    return pl.CostEstimate(flops=flops, bytes_accessed=moved, transcendentals=0)


def exchange(away, beside):
    count = lax.axis_size("tile")
    pairs = [(i, i + 1) for i in range(1, count - 1, 2)]
    there = lax.ppermute(away, "tile", pairs + [(b, a) for a, b in pairs])
    return there, swap(beside)


def swap(value):
    count = lax.axis_size("tile")
    return lax.ppermute(value, "tile", [(i, i ^ 1) for i in range(count)])


def two_terms(plane):
    top = plane.astype(BF)
    return [top, (plane - lax.reduce_precision(plane, 8, 7)).astype(BF)]


def local(
    background_prev,
    background_now,
    stiffness,
    drift_terms,
    born_prev,
    born_now,
    pieces,
    piece_target,
    piece_block,
    wavelet,
    source_cell,
    receiver_z,
    receiver_x,
    receiver_y,
):
    tiles = lax.axis_size("tile")
    place = lax.axis_index("tile")
    k = born_now.shape[0]
    depth, nx, ny = background_now.shape
    zb = pieces.shape[2]

    odd = place % 2
    packed = pack(pieces, piece_target[:, 0], piece_block, tiles)
    incoming = lax.all_to_all(packed, "tile", 0, 0, tiled=True)

    def face(planes):
        near = two_terms(background_now[:, planes[0], :])
        rows = near + [background_now[:, p, :].astype(BF) for p in planes[1:]]
        born = jnp.stack([born_now[:, :, p, :] for p in planes], axis=1)
        return jnp.concatenate([jnp.stack(rows), born.reshape(k * 4, depth, ny)])

    low, high = face((0, 1, 2, 3)), face((7, 6, 5, 4))
    low_in, high_in = exchange(jnp.where(odd == 0, low, high), jnp.where(odd == 0, high, low))

    where = jnp.stack([place * nx, jnp.int32(nx), jnp.int32(depth)]).astype(jnp.int32)
    rec = list_receivers(receiver_z, receiver_x, receiver_y, where)
    src = jnp.stack([source_cell[0], source_cell[1] - place * nx, source_cell[2], odd])

    def planes_first(background, born):
        return jnp.concatenate(
            [
                background.transpose(1, 0, 2)[None],
                born.astype(F32).transpose(0, 2, 1, 3),
            ]
        )

    cur = planes_first(background_now, born_now)
    prev = planes_first(background_prev, born_prev)
    coef = jnp.concatenate(
        [
            (stiffness.astype(F32) * (1.0 / 5040.0))[None],
            drift_terms.astype(F32) * (1.0 / 840.0),
        ]
    ).transpose(0, 2, 1, 3)
    taps = jnp.asarray(tap_matrix(ny)).astype(BF)

    state = jax.ShapeDtypeStruct((F, nx, depth, ny), F32)
    field = jax.ShapeDtypeStruct((nx, depth, ny), F32)
    faces = jax.ShapeDtypeStruct((5 * F, depth, ny), BF)
    wider = jax.ShapeDtypeStruct((5 * F + 1, depth, ny), BF)
    traced = jax.ShapeDtypeStruct((2, 8, 128), F32)
    small = VM((8, 128), F32)
    pair = VM((2, 8, 128), F32)
    work = [VM((nx + 8, depth + 16, ny), F32), VM((nx, depth, 2 * ny), F32)]
    cells = F * nx * depth * ny

    def call(kernel, name, out_shape, scratch, scalars, arrays, flops, spec=vspec(), mib=16):
        return pl.pallas_call(
            kernel,
            out_shape=out_shape,
            in_specs=[sspec()] * len(scalars) + [spec] * len(arrays),
            out_specs=tuple(vspec() for _ in out_shape),
            scratch_shapes=scratch,
            compiler_params=params(mib),
            cost_estimate=cost(flops * cells, 16 * cells),
            name=name,
        )(*scalars, *arrays)

    records = []
    perturb = table = found = None
    for n in range(ITERS):
        name = "own%d" % (n + 1)
        start = (wavelet, src)
        arrays = (cur, prev, coef, taps)
        if n == 1:
            part, acc, table = call(
                functools.partial(own_table_kernel, n),
                name,
                (state, field, jax.ShapeDtypeStruct((64, 128), BF)),
                work + [small, pair],
                start + (rec,),
                arrays + (perturb,),
                80,
            )
        elif n == ITERS - 1:
            (mine,) = call(
                share_kernel,
                "share",
                (jax.ShapeDtypeStruct((8, 128), F32),),
                [small] * 6 + [pair] * 6,
                (rec,),
                (cur, prev, coef, perturb, found),
                20,
            )
            part, acc = call(
                functools.partial(own_kernel, n), name, (state, field), work, start, arrays, 80000
            )
        else:
            part, acc = call(
                functools.partial(own_kernel, n),
                name,
                (state, field),
                work,
                start,
                arrays,
                80,
            )
        arrays = (part, acc, low_in, high_in, coef)
        name = "finish%d" % (n + 1)
        keep = VM((nx, depth, ny), F32)
        if n == 0:
            nxt, perturb, low, high, traces = call(
                gather_kernel,
                name,
                (state, jax.ShapeDtypeStruct((k, nx, depth, ny), F32), faces, faces, traced),
                [VM(a.shape, a.dtype) for a in arrays + (incoming,)]
                + [
                    keep,
                    small,
                    VM((tiles, 128), jnp.int32),
                    SM((tiles, 128), jnp.int32),
                    pltpu.SemaphoreType.DMA,
                    pltpu.SemaphoreType.DMA((6,)),
                ],
                (src, rec),
                arrays + (incoming,),
                20,
                pl.BlockSpec(memory_space=pltpu.HBM),
                58,
            )
        elif n == ITERS - 1:
            (born,) = call(
                functools.partial(finish_kernel, n),
                name,
                (jax.ShapeDtypeStruct((k, depth * nx, ny), F32),),
                [keep],
                (src,),
                arrays + (perturb,),
                20,
            )
            break
        else:
            face_type = wider if n == 1 else faces
            more = () if n == 1 else (jax.ShapeDtypeStruct((16, 128), F32),)
            nxt, low, high, traces, *more = call(
                functools.partial(finish_kernel, n),
                name,
                (state, face_type, face_type, traced) + more,
                [keep, small],
                (src, rec),
                arrays + (perturb,) + ((table,) if n == 1 else ()),
                20,
            )
            if n == 2:
                (found,) = more
        records.append(traces)
        low_in, high_in = exchange(low, high)
        prev, cur = cur, nxt

    early = jnp.stack([records[0] + records[1], records[2]])
    early = early + swap(early)
    half = jnp.where(odd == 0, early[0], early[1])
    message = jnp.concatenate([half, mine[None]])
    groups = [list(range(c, tiles, 2)) for c in range(2)]
    copies = lax.all_to_all(
        jnp.broadcast_to(message[None], (tiles // 2,) + message.shape),
        "tile",
        0,
        0,
        axis_index_groups=groups,
        tiled=True,
    )
    copies, born = lax.optimization_barrier((copies, born))
    total = jnp.sum(copies, axis=0)
    other = swap(total)
    ours, theirs = total[:2], other[:2]
    first_two = jnp.where(odd == 0, ours, theirs).reshape(2, 2, k, 128)
    third = jnp.where(odd == 0, theirs, ours)[:, :k]
    fourth = (total[2] + other[2]).reshape(2, k, 128)
    steps = jnp.concatenate([first_two, third[:, None], fourth[:, None]], axis=1)
    traces = steps.transpose(2, 1, 0, 3).reshape(k, ITERS, 256)
    return born.reshape(k, depth, nx, ny), traces


def solution(mesh):
    placed = (
        P(None, "tile", None),
        P(None, "tile", None),
        P(None, "tile", None),
        P(None, None, "tile", None),
        P("dir", None, "tile", None),
        P("dir", None, "tile", None),
        P("dir", "tile", None, None),
        P("tile", None),
        P("tile"),
        P(),
        P(),
        P(),
        P(),
        P(),
    )
    return jax.shard_map(
        local,
        mesh=mesh,
        in_specs=placed,
        out_specs=(P("dir", None, "tile", None), P("dir", None, None)),
        check_vma=False,
    )
```

```python
import functools

import jax
import jax.numpy as jnp
import numpy as np
from jax import lax
from jax.experimental import pallas as pl
from jax.experimental.pallas import tpu as pltpu
from jax.sharding import PartitionSpec as P

ITERS = 4
CAP = 2
F = 5

CENTRE = -14350.0
SECOND = (0.0, 8064.0, -1008.0, 128.0, -9.0)
FIRST = (0.0, 672.0, -168.0, 32.0, -3.0)

BF = jnp.bfloat16
F32 = jnp.float32
VM = pltpu.VMEM
SM = pltpu.SMEM


def vspec():
    return pl.BlockSpec(memory_space=VM)


def sspec():
    return pl.BlockSpec(memory_space=SM)


def params(mib=16):
    return pltpu.CompilerParams(vmem_limit_bytes=mib * 1024 * 1024)


def tap_matrix(ny):
    both = np.zeros((ny, 2 * ny), np.float32)
    for k in range(1, 5):
        for y in range(ny):
            for at, sign in ((y + k, 1.0), (y - k, -1.0)):
                if 0 <= at < ny:
                    both[at, y] = SECOND[k]
                    both[at, ny + y] = sign * FIRST[k]
    return np.concatenate([both, both], axis=0)


def pack_kernel(target, block, pieces, packed, count, label):
    directions, rows, zb, ny = pieces.shape
    tiles = packed.shape[0]

    def clear(t, c):
        count[t] = 0
        for a in range(CAP):
            label[t * CAP + a] = 0
        return c

    lax.fori_loop(0, tiles, clear, 0)

    def place(r, c):
        t = target[r]
        a = count[t]
        count[t] = a + 1
        label[t * CAP + a] = block[r] + 1
        for k in range(directions):
            at = pl.multiple_of((a * directions + k) * zb, zb)
            packed[t, pl.ds(at, zb), :] = pieces[k, r]
        return c

    lax.fori_loop(0, rows, place, 0)
    lane_at = lax.broadcasted_iota(jnp.int32, (16, ny), 1)

    def name(t, c):
        held = jnp.zeros((16, ny), jnp.int32)
        for a in range(CAP):
            held = jnp.where(lane_at == a, label[t * CAP + a], held)
        packed[t, CAP * directions * zb :, :] = held.astype(F32).astype(BF)
        return c

    lax.fori_loop(0, tiles, name, 0)


def pack(pieces, target, block, tiles):
    k, rows, zb, ny = pieces.shape
    return pl.pallas_call(
        pack_kernel,
        out_shape=jax.ShapeDtypeStruct((tiles, CAP * k * zb + 16, ny), pieces.dtype),
        in_specs=[sspec(), sspec(), vspec()],
        out_specs=vspec(),
        scratch_shapes=[SM((tiles,), jnp.int32), SM((tiles * CAP,), jnp.int32)],
        compiler_params=params(),
        name="pack",
    )(target, block, pieces)


def list_kernel(rz, rx, ry, where, rec):
    first, planes, depth = where[0], where[1], where[2]

    def look(i, n):
        x = rx[i] - first
        inside = (x >= 0) & (x < planes)
        beside = (x >= -4) & (x < planes + 4) & jnp.logical_not(inside)

        @pl.when(inside)
        def _():
            rec[0, n[0]] = x * depth + rz[i]
            rec[1, n[0]] = ry[i]
            rec[2, n[0]] = i

        @pl.when(beside)
        def _():
            rec[3, n[1]] = (x + 4) * depth + rz[i]
            rec[4, n[1]] = ry[i]
            rec[5, n[1]] = i

        return n[0] + inside.astype(jnp.int32), n[1] + beside.astype(jnp.int32)

    inner, outer = lax.fori_loop(0, rz.shape[0], look, (jnp.int32(0), jnp.int32(0)))
    rec[6, 0] = inner
    rec[6, 1] = outer


def list_receivers(rz, rx, ry, where):
    n = rz.shape[0]
    return pl.pallas_call(
        list_kernel,
        out_shape=jax.ShapeDtypeStruct((8, n), jnp.int32),
        in_specs=[sspec()] * 4,
        out_specs=sspec(),
        compiler_params=params(),
        name="receivers",
    )(rz, rx, ry, where)


def at_receivers(rec, read, into, gathered):
    for target in into:
        target[...] = jnp.zeros(target.shape, F32)
    for g in gathered:
        g[...] = jnp.zeros(g.shape, F32)
    lane = lax.broadcasted_iota(jnp.int32, gathered[0].shape, 1)

    def one(j, c):
        row, y, at = rec[0, j], rec[1, j], rec[2, j]
        read(row, gathered)
        to = at % 128
        for g, target in zip(gathered, into):
            moved = pltpu.roll(g[...], (to - y + 128) % 128, 1)
            target[at // 128] = target[at // 128] + jnp.where(lane == to, moved, 0.0)
        return c

    lax.fori_loop(0, rec[6, 0], one, 0)


def apply_own(cur, f, buf, ybuf, taps, coef, emit):
    nx, depth, ny = cur.shape[1:]
    for x in range(nx):
        u = cur[f, x]
        buf[4 + x, 8 : 8 + depth] = u
        top = u.astype(BF)
        rest = (u - top.astype(F32)).astype(BF)
        ybuf[x] = jnp.dot(
            jnp.concatenate([top, rest], axis=1), taps[...], preferred_element_type=F32
        )
    rows = 32

    def part(i, c):
        x, h = i // (depth // rows), i % (depth // rows)
        z0 = pl.multiple_of(h * rows, rows)
        at = 8 + z0

        def rd(px, dz):
            return buf[px, pl.ds(at + dz, rows), :]

        u = rd(4 + x, 0)
        y = ybuf[x, pl.ds(z0, rows), :]
        second = (3.0 * CENTRE) * u + y[:, :ny]
        gx = gz = None
        for k in range(1, 5):
            p, m = rd(4 + x + k, 0), rd(4 + x - k, 0)
            second = second + SECOND[k] * (p + m)
            g = FIRST[k] * (p - m)
            gx = g if gx is None else gx + g
            p, m = rd(4 + x, k), rd(4 + x, -k)
            second = second + SECOND[k] * (p + m)
            g = FIRST[k] * (p - m)
            gz = g if gz is None else gz + g

        def cf(which):
            return coef[which, x, pl.ds(z0, rows), :]

        value = cf(0) * second + cf(1) * gz + cf(2) * gx + cf(3) * y[:, ny:]
        emit(x, z0, rows, u, value)
        return c

    lax.fori_loop(0, nx * (depth // rows), part, 0)


def clear_edges(buf, depth):
    nx = buf.shape[0] - 8
    for x in range(4):
        buf[x] = jnp.zeros(buf.shape[1:], F32)
        buf[4 + nx + x] = jnp.zeros(buf.shape[1:], F32)
    zeros = jnp.zeros((8, buf.shape[2]), F32)
    for x in range(nx):
        buf[4 + x, 0:8] = zeros
        buf[4 + x, 8 + depth : 16 + depth] = zeros


def source_term(n, wav, src, x, z0, shape):
    z = lax.broadcasted_iota(jnp.int32, shape, 0) + z0
    y = lax.broadcasted_iota(jnp.int32, shape, 1)
    at = (z == src[0]) & (y == src[2])
    amount = jnp.where(x == src[1], wav[n], 0.0)
    return jnp.where(at, amount, 0.0)


def own_part(n, wav, src, cur, prev, coef, taps, part, acc, buf, ybuf):
    depth = cur.shape[2]
    clear_edges(buf, depth)
    for f in range(F):

        def emit(x, z0, rows, u, value, f=f):
            rs = pl.ds(z0, rows)
            new = 2.0 * u - prev[f, x, rs, :] + value
            if f == 0:
                acc[x, rs, :] = value
                new = new + source_term(n, wav, src, x, z0, u.shape)
            part[f, x, rs, :] = new

        apply_own(cur, f, buf, ybuf, taps, coef, emit)


def own_kernel(n, wav, src, cur, prev, coef, taps, part, acc, buf, ybuf):
    own_part(n, wav, src, cur, prev, coef, taps, part, acc, buf, ybuf)


def own_table_kernel(
    n, wav, src, *refs
):
    rec, cur, prev, coef, taps, perturb, part, acc, table, buf, ybuf, gathered, found = refs
    own_part(n, wav, src, cur, prev, coef, taps, part, acc, buf, ybuf)
    k, nx, depth, ny = perturb.shape

    def read(row, gs):
        x, z = row // depth, pl.ds(row % depth, 1)
        gs[0][0:1, :] = coef[0, x, z, :]
        gs[0][1:2, :] = coef[2, x, z, :]
        for j in range(k):
            gs[0][2 + j : 3 + j, :] = perturb[j, x, z, :]

    at_receivers(rec, read, [found], [gathered])
    left = found[...].reshape(16, 128)
    for term in range(3):
        rounded = left.astype(BF)
        table[16 * term : 16 * term + 16, :] = rounded
        left = left - rounded.astype(F32)
    table[48:64, :] = jnp.zeros((16, 128), BF)


def share_kernel(*refs):
    rec, cur, prev, coef, perturb, table, traces = refs[:7]
    gathered, found = refs[7:13], refs[13:19]
    k, nx, depth, ny = perturb.shape
    lane = lax.broadcasted_iota(jnp.int32, (8, 128), 1)
    for ref in gathered + found:
        ref[...] = jnp.zeros(ref.shape, F32)

    g2, g1 = gathered[:2]
    t2, t1 = found[:2]

    def beside(i, c):
        row, y, at = rec[3, i], rec[4, i], rec[5, i]
        x, z = row // depth - 4, pl.ds(row % depth, 1)
        near = jnp.where(x < 0, 0, nx - 4)
        weights = []
        for q in range(4):
            d = near + q - x
            away = jnp.abs(d)
            c2 = c1 = jnp.float32(0.0)
            for t in range(1, 5):
                c2 = jnp.where(away == t, jnp.float32(SECOND[t]), c2)
                c1 = jnp.where(away == t, jnp.float32(FIRST[t]), c1)
            weights.append((c2, jnp.where(d < 0, -c1, c1)))
        for f in range(F):
            second = first = jnp.zeros((1, ny), F32)
            for q in range(4):
                u = cur[f, near + q, z, :]
                second = second + weights[q][0] * u
                first = first + weights[q][1] * u
            g2[f : f + 1, :] = second
            g1[f : f + 1, :] = first
        to = at % 128
        shift = (to - y + 128) % 128
        here = lane == to
        h = at // 128
        t2[h] = t2[h] + jnp.where(here, pltpu.roll(g2[...], shift, 1), 0.0)
        t1[h] = t1[h] + jnp.where(here, pltpu.roll(g1[...], shift, 1), 0.0)
        return c

    lax.fori_loop(0, rec[6, 1], beside, 0)
    for h in range(2):
        const = table[8 * h : 8 * h + 8, :]
        reach = const[0:1] * t2[h] + const[1:2] * t1[h]
        for j in range(k):
            traces[h * k + j : h * k + j + 1, :] = (
                reach[1 + j : 2 + j] + const[2 + j : 3 + j] * reach[0:1]
            )

    for ref in found:
        ref[...] = jnp.zeros(ref.shape, F32)
    gs, gz, gx, gu, gp, gc = gathered
    fs, fz, fx, fy, fu, fc = found

    def inside(at, size, weight):
        return jnp.where((at >= 0) & (at < size), jnp.float32(weight), jnp.float32(0.0))

    def own(i, c):
        row, y, at = rec[0, i], rec[1, i], rec[2, i]
        x, z = row // depth, row % depth
        here_z = pl.ds(z, 1)
        reach = []
        for d in (1, 2, 3, 4, -1, -2, -3, -4):
            t = abs(d)
            sign = 1.0 if d > 0 else -1.0
            px, pz = jnp.clip(x + d, 0, nx - 1), jnp.clip(z + d, 0, depth - 1)
            reach.append(
                (
                    px,
                    inside(x + d, nx, SECOND[t]),
                    inside(x + d, nx, sign * FIRST[t]),
                    pl.ds(pz, 1),
                    inside(z + d, depth, SECOND[t]),
                    inside(z + d, depth, sign * FIRST[t]),
                )
            )
        for f in range(F):
            u = cur[f, x, here_z, :]
            second = (3.0 * CENTRE) * u
            along_x = along_z = jnp.zeros((1, ny), F32)
            for px, x2, x1, pz, z2, z1 in reach:
                v = cur[f, px, here_z, :]
                w = cur[f, x, pz, :]
                second = second + x2 * v + z2 * w
                along_x = along_x + x1 * v
                along_z = along_z + z1 * w
            gs[f : f + 1, :] = second
            gz[f : f + 1, :] = along_z
            gx[f : f + 1, :] = along_x
            gu[f : f + 1, :] = u
            gp[f : f + 1, :] = 2.0 * u - prev[f, x, here_z, :]
        for a in range(4):
            gc[a : a + 1, :] = coef[a, x, here_z, :]
        for j in range(k):
            gc[4 + j : 5 + j, :] = perturb[j, x, here_z, :]
        to = at % 128
        shift = to - y + 256
        here = lane == to
        h = at // 128

        def moved(ref, by=0):
            return pltpu.roll(ref[...], (shift - by) % 128, 1)

        second, along_y = moved(gs), jnp.zeros((8, 128), F32)
        for d in (1, 2, 3, 4, -1, -2, -3, -4):
            t = abs(d)
            v = moved(gu, d)
            second = second + inside(y + d, ny, SECOND[t]) * v
            along_y = along_y + inside(y + d, ny, FIRST[t] if d > 0 else -FIRST[t]) * v
        for ref, value in (
            (fs, second),
            (fz, moved(gz)),
            (fx, moved(gx)),
            (fy, along_y),
            (fu, moved(gp)),
            (fc, moved(gc)),
        ):
            ref[h] = ref[h] + jnp.where(here, value, 0.0)
        return c

    lax.fori_loop(0, rec[6, 0], own, 0)
    for h in range(2):
        con = fc[h]
        value = con[0:1] * fs[h] + con[1:2] * fz[h] + con[2:3] * fx[h] + con[3:4] * fy[h]
        base = fu[h] + value
        for j in range(k):
            at = slice(h * k + j, h * k + j + 1)
            traces[at, :] = (
                traces[at, :] + base[1 + j : 2 + j] + con[4 + j : 5 + j] * value[0:1]
            )


def near_planes(msg, f, first, rs):
    if first and f > 0:
        base = 5 + 4 * (f - 1)
        return [msg[base + p, rs, :].astype(F32) for p in range(4)]
    base = 5 * f
    near = msg[base, rs, :].astype(F32) + msg[base + 1, rs, :].astype(F32)
    return [near] + [msg[base + 1 + p, rs, :].astype(F32) for p in range(1, 4)]


def send_plane(msg, f, p, rs, new):
    top = new.astype(BF)
    if p == 0:
        msg[5 * f, rs, :] = top
        msg[5 * f + 1, rs, :] = (new - top.astype(F32)).astype(BF)
    else:
        msg[5 * f + 1 + p, rs, :] = top


def finish_part(n, part, acc_own, low_in, high_in, coef, perturb, acc, nxt, low, high, out):
    nx, depth, ny = part.shape[1:]
    rows = 16
    last = n == ITERS - 1
    for f in range(F):

        def piece(i, c, f=f):
            z0 = pl.multiple_of(i * rows, rows)
            rs = pl.ds(z0, rows)
            below = near_planes(low_in, f, n == 0, rs)
            above = near_planes(high_in, f, n == 0, rs)
            for x in range(nx):
                lower = x < 4
                planes, d, sign = (below, x, -1.0) if lower else (above, nx - 1 - x, 1.0)
                second = first = None
                for j in range(4 - d):
                    t = d + 1 + j
                    s, g = SECOND[t] * planes[j], (sign * FIRST[t]) * planes[j]
                    second = s if second is None else second + s
                    first = g if first is None else first + g
                reach = coef[0, x, rs, :] * second + coef[2, x, rs, :] * first
                if f == 0:
                    acc[x, rs, :] = acc_own[x, rs, :] + reach
                    if last:
                        continue
                    new = part[f, x, rs, :] + reach
                else:
                    new = part[f, x, rs, :] + reach + perturb[f - 1, x, rs, :] * acc[x, rs, :]
                if last:
                    out[f - 1, pl.ds(z0 * nx + x, rows, stride=nx), :] = new
                else:
                    nxt[f, x, rs, :] = new
                    send_plane(low if lower else high, f, d, rs, new)
            return c

        lax.fori_loop(0, depth // rows, piece, 0)


def by_parity(odd, run):
    @pl.when(odd == 0)
    def _():
        run(True)

    @pl.when(odd == 1)
    def _():
        run(False)


def sample_new(n, rec, nxt, traces, gathered, depth, k):
    offset = (n % 2) * k

    def read(row, gs):
        for j in range(k):
            gs[0][offset + j : offset + j + 1, :] = nxt[
                j + 1, row // depth, pl.ds(row % depth, 1), :
            ]

    at_receivers(rec, read, [traces], [gathered])


def gather_kernel(*refs):
    src, rec = refs[:2]
    far = refs[2:8]
    nxt, perturb, away, beside, traces = refs[8:13]
    near = refs[13:19]
    acc, gathered, names, labels, arrived, landed = refs[19:]
    loads = [pltpu.make_async_copy(a, b, landed.at[i]) for i, (a, b) in enumerate(zip(far, near))]
    for load in reversed(loads):
        load.start()
    part, acc_own, away_in, beside_in, coef, incoming = near
    k, nx, depth, ny = perturb.shape
    loads[5].wait()
    zb = (incoming.shape[1] - 16) // (CAP * k)
    for t in range(incoming.shape[0]):
        names[t : t + 1, :] = (
            incoming[t, CAP * k * zb : CAP * k * zb + 16, :].astype(F32)[0:1].astype(jnp.int32)
        )
    copy = pltpu.make_async_copy(names, labels, arrived)
    copy.start()
    perturb[...] = jnp.zeros(perturb.shape, F32)
    copy.wait()

    def add(s, c):
        t, a = s // CAP, s % CAP
        label = labels[t, a]

        @pl.when(label > 0)
        def _():
            b = label - 1
            x = b % nx
            z0 = pl.multiple_of((b // nx) * zb, zb)
            for j in range(k):
                at = pl.multiple_of((a * k + j) * zb, zb)
                perturb[j, x, pl.ds(z0, zb), :] = perturb[j, x, pl.ds(z0, zb), :] + incoming[
                    t, pl.ds(at, zb), :
                ].astype(F32)

        return c

    lax.fori_loop(0, incoming.shape[0] * CAP, add, 0)
    for load in loads[:5]:
        load.wait()

    def run(even):
        low_in, high_in = (away_in, beside_in) if even else (beside_in, away_in)
        low, high = (away, beside) if even else (beside, away)
        finish_part(0, part, acc_own, low_in, high_in, coef, perturb, acc, nxt, low, high, None)

    by_parity(src[3], run)
    sample_new(0, rec, nxt, traces, gathered, depth, k)


def finish_kernel(n, src, *refs):
    last = n == ITERS - 1
    rec = None
    if not last:
        rec, refs = refs[0], refs[1:]
    part, acc_own, away_in, beside_in, coef, perturb = refs[:6]
    rest = refs[6:]
    k, nx, depth, ny = perturb.shape
    out = nxt = away = beside = None
    if last:
        out, acc = rest
    elif n == 1:
        table, nxt, away, beside, traces, acc, gathered = rest
        away[5 * F] = table[...]
        beside[5 * F] = table[...]
    else:
        nxt, away, beside, traces, found, acc, gathered = rest
        both = jnp.zeros((16, 128), F32)
        for msg in (away_in, beside_in):
            for term in range(3):
                both = both + msg[5 * F, 16 * term : 16 * term + 16, :].astype(F32)
        found[...] = both

    def run(even):
        low_in, high_in = (away_in, beside_in) if even else (beside_in, away_in)
        low, high = (away, beside) if even else (beside, away)
        finish_part(n, part, acc_own, low_in, high_in, coef, perturb, acc, nxt, low, high, out)

    by_parity(src[3], run)
    if not last:
        sample_new(n, rec, nxt, traces, gathered, depth, k)


def cost(flops, moved):
    return pl.CostEstimate(flops=flops, bytes_accessed=moved, transcendentals=0)


def exchange(away, beside):
    count = lax.axis_size("tile")
    pairs = [(i, i + 1) for i in range(1, count - 1, 2)]
    there = lax.ppermute(away, "tile", pairs + [(b, a) for a, b in pairs])
    return there, swap(beside)


def swap(value):
    count = lax.axis_size("tile")
    return lax.ppermute(value, "tile", [(i, i ^ 1) for i in range(count)])


def two_terms(plane):
    top = plane.astype(BF)
    return [top, (plane - lax.reduce_precision(plane, 8, 7)).astype(BF)]


def local(
    background_prev,
    background_now,
    stiffness,
    drift_terms,
    born_prev,
    born_now,
    pieces,
    piece_target,
    piece_block,
    wavelet,
    source_cell,
    receiver_z,
    receiver_x,
    receiver_y,
):
    tiles = lax.axis_size("tile")
    place = lax.axis_index("tile")
    k = born_now.shape[0]
    depth, nx, ny = background_now.shape
    zb = pieces.shape[2]

    odd = place % 2
    packed = pack(pieces, piece_target[:, 0], piece_block, tiles)
    incoming = lax.all_to_all(packed, "tile", 0, 0, tiled=True)

    def face(planes):
        near = two_terms(background_now[:, planes[0], :])
        rows = near + [background_now[:, p, :].astype(BF) for p in planes[1:]]
        born = jnp.stack([born_now[:, :, p, :] for p in planes], axis=1)
        return jnp.concatenate([jnp.stack(rows), born.reshape(k * 4, depth, ny)])

    low, high = face((0, 1, 2, 3)), face((7, 6, 5, 4))
    low_in, high_in = exchange(jnp.where(odd == 0, low, high), jnp.where(odd == 0, high, low))

    where = jnp.stack([place * nx, jnp.int32(nx), jnp.int32(depth)]).astype(jnp.int32)
    rec = list_receivers(receiver_z, receiver_x, receiver_y, where)
    src = jnp.stack([source_cell[0], source_cell[1] - place * nx, source_cell[2], odd])

    def planes_first(background, born):
        return jnp.concatenate(
            [
                background.transpose(1, 0, 2)[None],
                born.astype(F32).transpose(0, 2, 1, 3),
            ]
        )

    cur = planes_first(background_now, born_now)
    prev = planes_first(background_prev, born_prev)
    coef = jnp.concatenate(
        [
            (stiffness.astype(F32) * (1.0 / 5040.0))[None],
            drift_terms.astype(F32) * (1.0 / 840.0),
        ]
    ).transpose(0, 2, 1, 3)
    taps = jnp.asarray(tap_matrix(ny)).astype(BF)

    state = jax.ShapeDtypeStruct((F, nx, depth, ny), F32)
    field = jax.ShapeDtypeStruct((nx, depth, ny), F32)
    faces = jax.ShapeDtypeStruct((5 * F, depth, ny), BF)
    wider = jax.ShapeDtypeStruct((5 * F + 1, depth, ny), BF)
    traced = jax.ShapeDtypeStruct((2, 8, 128), F32)
    small = VM((8, 128), F32)
    pair = VM((2, 8, 128), F32)
    work = [VM((nx + 8, depth + 16, ny), F32), VM((nx, depth, 2 * ny), F32)]
    cells = F * nx * depth * ny

    def call(kernel, name, out_shape, scratch, scalars, arrays, flops, spec=vspec(), mib=16):
        return pl.pallas_call(
            kernel,
            out_shape=out_shape,
            in_specs=[sspec()] * len(scalars) + [spec] * len(arrays),
            out_specs=tuple(vspec() for _ in out_shape),
            scratch_shapes=scratch,
            compiler_params=params(mib),
            cost_estimate=cost(flops * cells, 16 * cells),
            name=name,
        )(*scalars, *arrays)

    records = []
    perturb = table = found = None
    for n in range(ITERS):
        name = "own%d" % (n + 1)
        start = (wavelet, src)
        arrays = (cur, prev, coef, taps)
        if n == 1:
            part, acc, table = call(
                functools.partial(own_table_kernel, n),
                name,
                (state, field, jax.ShapeDtypeStruct((64, 128), BF)),
                work + [small, pair],
                start + (rec,),
                arrays + (perturb,),
                80,
            )
        elif n == ITERS - 1:
            (mine,) = call(
                share_kernel,
                "share",
                (jax.ShapeDtypeStruct((8, 128), F32),),
                [small] * 6 + [pair] * 6,
                (rec,),
                (cur, prev, coef, perturb, found),
                20,
            )
            part, acc = call(
                functools.partial(own_kernel, n), name, (state, field), work, start, arrays, 80000
            )
            message = jnp.concatenate([records[0] + records[1], records[2][:, :k].reshape(1, 8, 128), mine[None]])
            groups = [list(range(c, tiles, 2)) for c in range(2)]
            copies = lax.all_to_all(
                jnp.broadcast_to(message[None], (tiles // 2,) + message.shape),
                "tile",
                0,
                0,
                axis_index_groups=groups,
                tiled=True,
            )
            copies, part, acc = lax.optimization_barrier((copies, part, acc))
            total = jnp.sum(copies, axis=0)
            total = total + swap(total)
            first_two = total[:2].reshape(2, 2, k, 128)
            rest = total[2:].reshape(2, 2, k, 128).transpose(1, 0, 2, 3)
            steps = jnp.concatenate([first_two, rest], axis=1)
            traces = steps.transpose(2, 1, 0, 3).reshape(k, ITERS, 256)
            part, traces = lax.optimization_barrier((part, traces))
        else:
            part, acc = call(
                functools.partial(own_kernel, n),
                name,
                (state, field),
                work,
                start,
                arrays,
                80,
            )
        arrays = (part, acc, low_in, high_in, coef)
        name = "finish%d" % (n + 1)
        keep = VM((nx, depth, ny), F32)
        if n == 0:
            nxt, perturb, low, high, traces = call(
                gather_kernel,
                name,
                (state, jax.ShapeDtypeStruct((k, nx, depth, ny), F32), faces, faces, traced),
                [VM(a.shape, a.dtype) for a in arrays + (incoming,)]
                + [
                    keep,
                    small,
                    VM((tiles, 128), jnp.int32),
                    SM((tiles, 128), jnp.int32),
                    pltpu.SemaphoreType.DMA,
                    pltpu.SemaphoreType.DMA((6,)),
                ],
                (src, rec),
                arrays + (incoming,),
                20,
                pl.BlockSpec(memory_space=pltpu.HBM),
                58,
            )
        elif n == ITERS - 1:
            (born,) = call(
                functools.partial(finish_kernel, n),
                name,
                (jax.ShapeDtypeStruct((k, depth * nx, ny), F32),),
                [keep],
                (src,),
                arrays + (perturb,),
                20,
            )
            break
        else:
            face_type = wider if n == 1 else faces
            more = () if n == 1 else (jax.ShapeDtypeStruct((16, 128), F32),)
            nxt, low, high, traces, *more = call(
                functools.partial(finish_kernel, n),
                name,
                (state, face_type, face_type, traced) + more,
                [keep, small],
                (src, rec),
                arrays + (perturb,) + ((table,) if n == 1 else ()),
                20,
            )
            if n == 2:
                (found,) = more
        records.append(traces)
        low_in, high_in = exchange(low, high)
        prev, cur = cur, nxt

    return born.reshape(k, depth, nx, ny), traces


def solution(mesh):
    placed = (
        P(None, "tile", None),
        P(None, "tile", None),
        P(None, "tile", None),
        P(None, None, "tile", None),
        P("dir", None, "tile", None),
        P("dir", None, "tile", None),
        P("dir", "tile", None, None),
        P("tile", None),
        P("tile"),
        P(),
        P(),
        P(),
        P(),
        P(),
    )
    return jax.shard_map(
        local,
        mesh=mesh,
        in_specs=placed,
        out_specs=(P("dir", None, "tile", None), P("dir", None, None)),
        check_vma=False,
    )
```

```python
import functools

import jax
import jax.numpy as jnp
import numpy as np
from jax import lax
from jax.experimental import pallas as pl
from jax.experimental.pallas import tpu as pltpu
from jax.sharding import PartitionSpec as P

ITERS = 4
CAP = 2
F = 5

CENTRE = -14350.0
SECOND = (0.0, 8064.0, -1008.0, 128.0, -9.0)
FIRST = (0.0, 672.0, -168.0, 32.0, -3.0)

BF = jnp.bfloat16
F32 = jnp.float32
VM = pltpu.VMEM
SM = pltpu.SMEM


def vspec():
    return pl.BlockSpec(memory_space=VM)


def sspec():
    return pl.BlockSpec(memory_space=SM)


def params(mib=16):
    return pltpu.CompilerParams(vmem_limit_bytes=mib * 1024 * 1024)


def tap_matrix(ny):
    both = np.zeros((ny, 2 * ny), np.float32)
    for k in range(1, 5):
        for y in range(ny):
            for at, sign in ((y + k, 1.0), (y - k, -1.0)):
                if 0 <= at < ny:
                    both[at, y] = SECOND[k]
                    both[at, ny + y] = sign * FIRST[k]
    return np.concatenate([both, both], axis=0)


def pack_kernel(target, block, pieces, packed, count, label):
    directions, rows, zb, ny = pieces.shape
    tiles = packed.shape[0]

    def clear(t, c):
        count[t] = 0
        for a in range(CAP):
            label[t * CAP + a] = 0
        return c

    lax.fori_loop(0, tiles, clear, 0)

    def place(r, c):
        t = target[r]
        a = count[t]
        count[t] = a + 1
        label[t * CAP + a] = block[r] + 1
        for k in range(directions):
            at = pl.multiple_of((a * directions + k) * zb, zb)
            packed[t, pl.ds(at, zb), :] = pieces[k, r]
        return c

    lax.fori_loop(0, rows, place, 0)
    lane_at = lax.broadcasted_iota(jnp.int32, (16, ny), 1)

    def name(t, c):
        held = jnp.zeros((16, ny), jnp.int32)
        for a in range(CAP):
            held = jnp.where(lane_at == a, label[t * CAP + a], held)
        packed[t, CAP * directions * zb :, :] = held.astype(F32).astype(BF)
        return c

    lax.fori_loop(0, tiles, name, 0)


def pack(pieces, target, block, tiles):
    k, rows, zb, ny = pieces.shape
    return pl.pallas_call(
        pack_kernel,
        out_shape=jax.ShapeDtypeStruct((tiles, CAP * k * zb + 16, ny), pieces.dtype),
        in_specs=[sspec(), sspec(), vspec()],
        out_specs=vspec(),
        scratch_shapes=[SM((tiles,), jnp.int32), SM((tiles * CAP,), jnp.int32)],
        compiler_params=params(),
        name="pack",
    )(target, block, pieces)


def list_kernel(rz, rx, ry, where, rec):
    first, planes, depth = where[0], where[1], where[2]

    def look(i, n):
        x = rx[i] - first
        inside = (x >= 0) & (x < planes)
        beside = (x >= -4) & (x < planes + 4) & jnp.logical_not(inside)

        @pl.when(inside)
        def _():
            rec[0, n[0]] = x * depth + rz[i]
            rec[1, n[0]] = ry[i]
            rec[2, n[0]] = i

        @pl.when(beside)
        def _():
            rec[3, n[1]] = (x + 4) * depth + rz[i]
            rec[4, n[1]] = ry[i]
            rec[5, n[1]] = i

        return n[0] + inside.astype(jnp.int32), n[1] + beside.astype(jnp.int32)

    inner, outer = lax.fori_loop(0, rz.shape[0], look, (jnp.int32(0), jnp.int32(0)))
    rec[6, 0] = inner
    rec[6, 1] = outer


def list_receivers(rz, rx, ry, where):
    n = rz.shape[0]
    return pl.pallas_call(
        list_kernel,
        out_shape=jax.ShapeDtypeStruct((8, n), jnp.int32),
        in_specs=[sspec()] * 4,
        out_specs=sspec(),
        compiler_params=params(),
        name="receivers",
    )(rz, rx, ry, where)


def at_receivers(rec, read, into, gathered):
    for target in into:
        target[...] = jnp.zeros(target.shape, F32)
    for g in gathered:
        g[...] = jnp.zeros(g.shape, F32)
    lane = lax.broadcasted_iota(jnp.int32, gathered[0].shape, 1)

    def one(j, c):
        row, y, at = rec[0, j], rec[1, j], rec[2, j]
        read(row, gathered)
        to = at % 128
        for g, target in zip(gathered, into):
            moved = pltpu.roll(g[...], (to - y + 128) % 128, 1)
            target[at // 128] = target[at // 128] + jnp.where(lane == to, moved, 0.0)
        return c

    lax.fori_loop(0, rec[6, 0], one, 0)


def apply_own(cur, f, buf, ybuf, taps, coef, emit):
    nx, depth, ny = cur.shape[1:]
    for x in range(nx):
        u = cur[f, x]
        buf[4 + x, 8 : 8 + depth] = u
        top = u.astype(BF)
        rest = (u - top.astype(F32)).astype(BF)
        ybuf[x] = jnp.dot(
            jnp.concatenate([top, rest], axis=1), taps[...], preferred_element_type=F32
        )
    rows = 32

    def part(i, c):
        x, h = i // (depth // rows), i % (depth // rows)
        z0 = pl.multiple_of(h * rows, rows)
        at = 8 + z0

        def rd(px, dz):
            return buf[px, pl.ds(at + dz, rows), :]

        u = rd(4 + x, 0)
        y = ybuf[x, pl.ds(z0, rows), :]
        second = (3.0 * CENTRE) * u + y[:, :ny]
        gx = gz = None
        for k in range(1, 5):
            p, m = rd(4 + x + k, 0), rd(4 + x - k, 0)
            second = second + SECOND[k] * (p + m)
            g = FIRST[k] * (p - m)
            gx = g if gx is None else gx + g
            p, m = rd(4 + x, k), rd(4 + x, -k)
            second = second + SECOND[k] * (p + m)
            g = FIRST[k] * (p - m)
            gz = g if gz is None else gz + g

        def cf(which):
            return coef[which, x, pl.ds(z0, rows), :]

        value = cf(0) * second + cf(1) * gz + cf(2) * gx + cf(3) * y[:, ny:]
        emit(x, z0, rows, u, value)
        return c

    lax.fori_loop(0, nx * (depth // rows), part, 0)


def clear_edges(buf, depth):
    nx = buf.shape[0] - 8
    for x in range(4):
        buf[x] = jnp.zeros(buf.shape[1:], F32)
        buf[4 + nx + x] = jnp.zeros(buf.shape[1:], F32)
    zeros = jnp.zeros((8, buf.shape[2]), F32)
    for x in range(nx):
        buf[4 + x, 0:8] = zeros
        buf[4 + x, 8 + depth : 16 + depth] = zeros


def source_term(n, wav, src, x, z0, shape):
    z = lax.broadcasted_iota(jnp.int32, shape, 0) + z0
    y = lax.broadcasted_iota(jnp.int32, shape, 1)
    at = (z == src[0]) & (y == src[2])
    amount = jnp.where(x == src[1], wav[n], 0.0)
    return jnp.where(at, amount, 0.0)


def own_part(n, wav, src, cur, prev, coef, taps, part, acc, buf, ybuf):
    depth = cur.shape[2]
    clear_edges(buf, depth)
    for f in range(F):

        def emit(x, z0, rows, u, value, f=f):
            rs = pl.ds(z0, rows)
            new = 2.0 * u - prev[f, x, rs, :] + value
            if f == 0:
                acc[x, rs, :] = value
                new = new + source_term(n, wav, src, x, z0, u.shape)
            part[f, x, rs, :] = new

        apply_own(cur, f, buf, ybuf, taps, coef, emit)


def own_kernel(n, wav, src, cur, prev, coef, taps, part, acc, buf, ybuf):
    own_part(n, wav, src, cur, prev, coef, taps, part, acc, buf, ybuf)


def own_table_kernel(
    n, wav, src, *refs
):
    rec, cur, prev, coef, taps, perturb, part, acc, table, buf, ybuf, gathered, found = refs
    own_part(n, wav, src, cur, prev, coef, taps, part, acc, buf, ybuf)
    k, nx, depth, ny = perturb.shape

    def read(row, gs):
        x, z = row // depth, pl.ds(row % depth, 1)
        gs[0][0:1, :] = coef[0, x, z, :]
        gs[0][1:2, :] = coef[2, x, z, :]
        for j in range(k):
            gs[0][2 + j : 3 + j, :] = perturb[j, x, z, :]

    at_receivers(rec, read, [found], [gathered])
    left = found[...].reshape(16, 128)
    for term in range(3):
        rounded = left.astype(BF)
        table[16 * term : 16 * term + 16, :] = rounded
        left = left - rounded.astype(F32)
    table[48:64, :] = jnp.zeros((16, 128), BF)


def share_kernel(*refs):
    rec, cur, prev, coef, perturb, table, traces = refs[:7]
    gathered, found = refs[7:13], refs[13:19]
    k, nx, depth, ny = perturb.shape
    lane = lax.broadcasted_iota(jnp.int32, (8, 128), 1)
    for ref in gathered + found:
        ref[...] = jnp.zeros(ref.shape, F32)

    g2, g1 = gathered[:2]
    t2, t1 = found[:2]

    def beside(i, c):
        row, y, at = rec[3, i], rec[4, i], rec[5, i]
        x, z = row // depth - 4, pl.ds(row % depth, 1)
        near = jnp.where(x < 0, 0, nx - 4)
        weights = []
        for q in range(4):
            d = near + q - x
            away = jnp.abs(d)
            c2 = c1 = jnp.float32(0.0)
            for t in range(1, 5):
                c2 = jnp.where(away == t, jnp.float32(SECOND[t]), c2)
                c1 = jnp.where(away == t, jnp.float32(FIRST[t]), c1)
            weights.append((c2, jnp.where(d < 0, -c1, c1)))
        for f in range(F):
            second = first = jnp.zeros((1, ny), F32)
            for q in range(4):
                u = cur[f, near + q, z, :]
                second = second + weights[q][0] * u
                first = first + weights[q][1] * u
            g2[f : f + 1, :] = second
            g1[f : f + 1, :] = first
        to = at % 128
        shift = (to - y + 128) % 128
        here = lane == to
        h = at // 128
        t2[h] = t2[h] + jnp.where(here, pltpu.roll(g2[...], shift, 1), 0.0)
        t1[h] = t1[h] + jnp.where(here, pltpu.roll(g1[...], shift, 1), 0.0)
        return c

    lax.fori_loop(0, rec[6, 1], beside, 0)
    for h in range(2):
        const = table[8 * h : 8 * h + 8, :]
        reach = const[0:1] * t2[h] + const[1:2] * t1[h]
        for j in range(k):
            traces[h * k + j : h * k + j + 1, :] = (
                reach[1 + j : 2 + j] + const[2 + j : 3 + j] * reach[0:1]
            )

    for ref in found:
        ref[...] = jnp.zeros(ref.shape, F32)
    gs, gz, gx, gu, gp, gc = gathered
    fs, fz, fx, fy, fu, fc = found

    def inside(at, size, weight):
        return jnp.where((at >= 0) & (at < size), jnp.float32(weight), jnp.float32(0.0))

    def own(i, c):
        row, y, at = rec[0, i], rec[1, i], rec[2, i]
        x, z = row // depth, row % depth
        here_z = pl.ds(z, 1)
        reach = []
        for d in (1, 2, 3, 4, -1, -2, -3, -4):
            t = abs(d)
            sign = 1.0 if d > 0 else -1.0
            px, pz = jnp.clip(x + d, 0, nx - 1), jnp.clip(z + d, 0, depth - 1)
            reach.append(
                (
                    px,
                    inside(x + d, nx, SECOND[t]),
                    inside(x + d, nx, sign * FIRST[t]),
                    pl.ds(pz, 1),
                    inside(z + d, depth, SECOND[t]),
                    inside(z + d, depth, sign * FIRST[t]),
                )
            )
        for f in range(F):
            u = cur[f, x, here_z, :]
            second = (3.0 * CENTRE) * u
            along_x = along_z = jnp.zeros((1, ny), F32)
            for px, x2, x1, pz, z2, z1 in reach:
                v = cur[f, px, here_z, :]
                w = cur[f, x, pz, :]
                second = second + x2 * v + z2 * w
                along_x = along_x + x1 * v
                along_z = along_z + z1 * w
            gs[f : f + 1, :] = second
            gz[f : f + 1, :] = along_z
            gx[f : f + 1, :] = along_x
            gu[f : f + 1, :] = u
            gp[f : f + 1, :] = 2.0 * u - prev[f, x, here_z, :]
        for a in range(4):
            gc[a : a + 1, :] = coef[a, x, here_z, :]
        for j in range(k):
            gc[4 + j : 5 + j, :] = perturb[j, x, here_z, :]
        to = at % 128
        shift = to - y + 256
        here = lane == to
        h = at // 128

        def moved(ref, by=0):
            return pltpu.roll(ref[...], (shift - by) % 128, 1)

        second, along_y = moved(gs), jnp.zeros((8, 128), F32)
        for d in (1, 2, 3, 4, -1, -2, -3, -4):
            t = abs(d)
            v = moved(gu, d)
            second = second + inside(y + d, ny, SECOND[t]) * v
            along_y = along_y + inside(y + d, ny, FIRST[t] if d > 0 else -FIRST[t]) * v
        for ref, value in (
            (fs, second),
            (fz, moved(gz)),
            (fx, moved(gx)),
            (fy, along_y),
            (fu, moved(gp)),
            (fc, moved(gc)),
        ):
            ref[h] = ref[h] + jnp.where(here, value, 0.0)
        return c

    lax.fori_loop(0, rec[6, 0], own, 0)
    for h in range(2):
        con = fc[h]
        value = con[0:1] * fs[h] + con[1:2] * fz[h] + con[2:3] * fx[h] + con[3:4] * fy[h]
        base = fu[h] + value
        for j in range(k):
            at = slice(h * k + j, h * k + j + 1)
            traces[at, :] = (
                traces[at, :] + base[1 + j : 2 + j] + con[4 + j : 5 + j] * value[0:1]
            )


def near_planes(msg, f, first, rs):
    if first and f > 0:
        base = 5 + 4 * (f - 1)
        return [msg[base + p, rs, :].astype(F32) for p in range(4)]
    base = 5 * f
    near = msg[base, rs, :].astype(F32) + msg[base + 1, rs, :].astype(F32)
    return [near] + [msg[base + 1 + p, rs, :].astype(F32) for p in range(1, 4)]


def send_plane(msg, f, p, rs, new):
    top = new.astype(BF)
    if p == 0:
        msg[5 * f, rs, :] = top
        msg[5 * f + 1, rs, :] = (new - top.astype(F32)).astype(BF)
    else:
        msg[5 * f + 1 + p, rs, :] = top


def finish_part(n, part, acc_own, low_in, high_in, coef, perturb, acc, nxt, low, high, out):
    nx, depth, ny = part.shape[1:]
    rows = 16
    last = n == ITERS - 1
    for f in range(F):

        def piece(i, c, f=f):
            z0 = pl.multiple_of(i * rows, rows)
            rs = pl.ds(z0, rows)
            below = near_planes(low_in, f, n == 0, rs)
            above = near_planes(high_in, f, n == 0, rs)
            for x in range(nx):
                lower = x < 4
                planes, d, sign = (below, x, -1.0) if lower else (above, nx - 1 - x, 1.0)
                second = first = None
                for j in range(4 - d):
                    t = d + 1 + j
                    s, g = SECOND[t] * planes[j], (sign * FIRST[t]) * planes[j]
                    second = s if second is None else second + s
                    first = g if first is None else first + g
                reach = coef[0, x, rs, :] * second + coef[2, x, rs, :] * first
                if f == 0:
                    acc[x, rs, :] = acc_own[x, rs, :] + reach
                    if last:
                        continue
                    new = part[f, x, rs, :] + reach
                else:
                    new = part[f, x, rs, :] + reach + perturb[f - 1, x, rs, :] * acc[x, rs, :]
                if last:
                    out[f - 1, pl.ds(z0 * nx + x, rows, stride=nx), :] = new
                else:
                    nxt[f, x, rs, :] = new
                    send_plane(low if lower else high, f, d, rs, new)
            return c

        lax.fori_loop(0, depth // rows, piece, 0)


def by_parity(odd, run):
    @pl.when(odd == 0)
    def _():
        run(True)

    @pl.when(odd == 1)
    def _():
        run(False)


def sample_new(n, rec, nxt, traces, gathered, depth, k):
    offset = (n % 2) * k

    def read(row, gs):
        for j in range(k):
            gs[0][offset + j : offset + j + 1, :] = nxt[
                j + 1, row // depth, pl.ds(row % depth, 1), :
            ]

    at_receivers(rec, read, [traces], [gathered])


def gather_kernel(*refs):
    src, rec = refs[:2]
    far = refs[2:8]
    nxt, perturb, away, beside, traces = refs[8:13]
    near = refs[13:19]
    acc, gathered, names, labels, arrived, landed = refs[19:]
    loads = [pltpu.make_async_copy(a, b, landed.at[i]) for i, (a, b) in enumerate(zip(far, near))]
    for load in reversed(loads):
        load.start()
    part, acc_own, away_in, beside_in, coef, incoming = near
    k, nx, depth, ny = perturb.shape
    loads[5].wait()
    zb = (incoming.shape[1] - 16) // (CAP * k)
    for t in range(incoming.shape[0]):
        names[t : t + 1, :] = (
            incoming[t, CAP * k * zb : CAP * k * zb + 16, :].astype(F32)[0:1].astype(jnp.int32)
        )
    copy = pltpu.make_async_copy(names, labels, arrived)
    copy.start()
    perturb[...] = jnp.zeros(perturb.shape, F32)
    copy.wait()

    def add(s, c):
        t, a = s // CAP, s % CAP
        label = labels[t, a]

        @pl.when(label > 0)
        def _():
            b = label - 1
            x = b % nx
            z0 = pl.multiple_of((b // nx) * zb, zb)
            for j in range(k):
                at = pl.multiple_of((a * k + j) * zb, zb)
                perturb[j, x, pl.ds(z0, zb), :] = perturb[j, x, pl.ds(z0, zb), :] + incoming[
                    t, pl.ds(at, zb), :
                ].astype(F32)

        return c

    lax.fori_loop(0, incoming.shape[0] * CAP, add, 0)
    for load in loads[:5]:
        load.wait()

    def run(even):
        low_in, high_in = (away_in, beside_in) if even else (beside_in, away_in)
        low, high = (away, beside) if even else (beside, away)
        finish_part(0, part, acc_own, low_in, high_in, coef, perturb, acc, nxt, low, high, None)

    by_parity(src[3], run)
    sample_new(0, rec, nxt, traces, gathered, depth, k)


def finish_kernel(n, src, *refs):
    last = n == ITERS - 1
    rec = None
    if not last:
        rec, refs = refs[0], refs[1:]
    part, acc_own, away_in, beside_in, coef, perturb = refs[:6]
    rest = refs[6:]
    k, nx, depth, ny = perturb.shape
    out = nxt = away = beside = None
    if last:
        out, acc = rest
    elif n == 1:
        table, nxt, away, beside, traces, acc, gathered = rest
        away[5 * F] = table[...]
        beside[5 * F] = table[...]
    else:
        early, nxt, away, beside, traces, found, acc, gathered = rest
        both = jnp.zeros((16, 128), F32)
        for msg in (away_in, beside_in):
            for term in range(3):
                both = both + msg[5 * F, 16 * term : 16 * term + 16, :].astype(F32)
        found[...] = both

    def run(even):
        low_in, high_in = (away_in, beside_in) if even else (beside_in, away_in)
        low, high = (away, beside) if even else (beside, away)
        finish_part(n, part, acc_own, low_in, high_in, coef, perturb, acc, nxt, low, high, out)

    by_parity(src[3], run)
    if last:
        return
    sample_new(n, rec, nxt, traces, gathered, depth, k)
    if n == 2:
        left = jnp.concatenate([early[...].reshape(16, 128), traces[...].reshape(16, 128)])
        for term in range(4):
            rounded = left.astype(BF) if term < 3 else jnp.zeros((32, 128), BF)
            beside[5 * F + term // 2, 32 * (term % 2) : 32 * (term % 2) + 32, :] = rounded
            left = left - rounded.astype(F32)


def message_kernel(src, beside, two, third, mine, out):
    own = jnp.concatenate([two[...].reshape(16, 128), third[...].reshape(16, 128)])
    theirs = beside[5 * F, 0:32, :].astype(F32) + beside[5 * F, 32:64, :].astype(F32)
    both = own + (theirs + beside[5 * F + 1, 0:32, :].astype(F32))
    half = jnp.where(src[3] == 0, both[0:16], both[16:32])
    message = jnp.concatenate([half, mine[...]]).reshape(3, 8, 128)
    for i in range(out.shape[0]):
        out[i] = message


def cost(flops, moved):
    return pl.CostEstimate(flops=flops, bytes_accessed=moved, transcendentals=0)


def exchange(away, beside):
    count = lax.axis_size("tile")
    pairs = [(i, i + 1) for i in range(1, count - 1, 2)]
    there = lax.ppermute(away, "tile", pairs + [(b, a) for a, b in pairs])
    return there, swap(beside)


def swap(value):
    count = lax.axis_size("tile")
    return lax.ppermute(value, "tile", [(i, i ^ 1) for i in range(count)])


def two_terms(plane):
    top = plane.astype(BF)
    return [top, (plane - lax.reduce_precision(plane, 8, 7)).astype(BF)]


def local(
    background_prev,
    background_now,
    stiffness,
    drift_terms,
    born_prev,
    born_now,
    pieces,
    piece_target,
    piece_block,
    wavelet,
    source_cell,
    receiver_z,
    receiver_x,
    receiver_y,
):
    tiles = lax.axis_size("tile")
    place = lax.axis_index("tile")
    k = born_now.shape[0]
    depth, nx, ny = background_now.shape
    zb = pieces.shape[2]

    odd = place % 2
    packed = pack(pieces, piece_target[:, 0], piece_block, tiles)
    incoming = lax.all_to_all(packed, "tile", 0, 0, tiled=True)

    def face(planes):
        near = two_terms(background_now[:, planes[0], :])
        rows = near + [background_now[:, p, :].astype(BF) for p in planes[1:]]
        born = jnp.stack([born_now[:, :, p, :] for p in planes], axis=1)
        return jnp.concatenate([jnp.stack(rows), born.reshape(k * 4, depth, ny)])

    low, high = face((0, 1, 2, 3)), face((7, 6, 5, 4))
    low_in, high_in = exchange(jnp.where(odd == 0, low, high), jnp.where(odd == 0, high, low))

    where = jnp.stack([place * nx, jnp.int32(nx), jnp.int32(depth)]).astype(jnp.int32)
    rec = list_receivers(receiver_z, receiver_x, receiver_y, where)
    src = jnp.stack([source_cell[0], source_cell[1] - place * nx, source_cell[2], odd])

    def planes_first(background, born):
        return jnp.concatenate(
            [
                background.transpose(1, 0, 2)[None],
                born.astype(F32).transpose(0, 2, 1, 3),
            ]
        )

    cur = planes_first(background_now, born_now)
    prev = planes_first(background_prev, born_prev)
    coef = jnp.concatenate(
        [
            (stiffness.astype(F32) * (1.0 / 5040.0))[None],
            drift_terms.astype(F32) * (1.0 / 840.0),
        ]
    ).transpose(0, 2, 1, 3)
    taps = jnp.asarray(tap_matrix(ny)).astype(BF)

    state = jax.ShapeDtypeStruct((F, nx, depth, ny), F32)
    field = jax.ShapeDtypeStruct((nx, depth, ny), F32)
    faces = jax.ShapeDtypeStruct((5 * F, depth, ny), BF)
    wider = jax.ShapeDtypeStruct((5 * F + 1, depth, ny), BF)
    widest = jax.ShapeDtypeStruct((5 * F + 2, depth, ny), BF)
    traced = jax.ShapeDtypeStruct((2, 8, 128), F32)
    small = VM((8, 128), F32)
    pair = VM((2, 8, 128), F32)
    work = [VM((nx + 8, depth + 16, ny), F32), VM((nx, depth, 2 * ny), F32)]
    cells = F * nx * depth * ny

    def call(kernel, name, out_shape, scratch, scalars, arrays, flops, spec=vspec(), mib=16):
        return pl.pallas_call(
            kernel,
            out_shape=out_shape,
            in_specs=[sspec()] * len(scalars) + [spec] * len(arrays),
            out_specs=tuple(vspec() for _ in out_shape),
            scratch_shapes=scratch,
            compiler_params=params(mib),
            cost_estimate=cost(flops * cells, 16 * cells),
            name=name,
        )(*scalars, *arrays)

    records = []
    perturb = table = found = None
    for n in range(ITERS):
        name = "own%d" % (n + 1)
        start = (wavelet, src)
        arrays = (cur, prev, coef, taps)
        if n == 1:
            part, acc, table = call(
                functools.partial(own_table_kernel, n),
                name,
                (state, field, jax.ShapeDtypeStruct((64, 128), BF)),
                work + [small, pair],
                start + (rec,),
                arrays + (perturb,),
                80,
            )
        elif n == ITERS - 1:
            (mine,) = call(
                share_kernel,
                "share",
                (jax.ShapeDtypeStruct((8, 128), F32),),
                [small] * 6 + [pair] * 6,
                (rec,),
                (cur, prev, coef, perturb, found),
                20,
            )
            part, acc = call(
                functools.partial(own_kernel, n), name, (state, field), work, start, arrays, 80000
            )
        else:
            part, acc = call(
                functools.partial(own_kernel, n),
                name,
                (state, field),
                work,
                start,
                arrays,
                80,
            )
        arrays = (part, acc, low_in, high_in, coef)
        name = "finish%d" % (n + 1)
        keep = VM((nx, depth, ny), F32)
        if n == 0:
            nxt, perturb, low, high, traces = call(
                gather_kernel,
                name,
                (state, jax.ShapeDtypeStruct((k, nx, depth, ny), F32), faces, faces, traced),
                [VM(a.shape, a.dtype) for a in arrays + (incoming,)]
                + [
                    keep,
                    small,
                    VM((tiles, 128), jnp.int32),
                    SM((tiles, 128), jnp.int32),
                    pltpu.SemaphoreType.DMA,
                    pltpu.SemaphoreType.DMA((6,)),
                ],
                (src, rec),
                arrays + (incoming,),
                20,
                pl.BlockSpec(memory_space=pltpu.HBM),
                58,
            )
        elif n == ITERS - 1:
            (born,) = call(
                functools.partial(finish_kernel, n),
                name,
                (jax.ShapeDtypeStruct((k, depth * nx, ny), F32),),
                [keep],
                (src,),
                arrays + (perturb,),
                20,
            )
            break
        else:
            face_type = wider if n == 1 else faces
            inner_type = wider if n == 1 else widest
            if n == 2:
                two = records[0] + records[1]
            extra = table if n == 1 else two
            more = () if n == 1 else (jax.ShapeDtypeStruct((16, 128), F32),)
            nxt, low, high, traces, *more = call(
                functools.partial(finish_kernel, n),
                name,
                (state, face_type, inner_type, traced) + more,
                [keep, small],
                (src, rec),
                arrays + (perturb, extra),
                20,
            )
            if n == 2:
                (found,) = more
        records.append(traces)
        low_in, high_in = exchange(low, high)
        prev, cur = cur, nxt

    (sent,) = call(
        message_kernel,
        "message",
        (jax.ShapeDtypeStruct((tiles // 2, 3, 8, 128), F32),),
        [],
        (src,),
        (high_in, two, records[2], mine),
        1,
    )
    groups = [list(range(c, tiles, 2)) for c in range(2)]
    copies = lax.all_to_all(
        sent,
        "tile",
        0,
        0,
        axis_index_groups=groups,
        tiled=True,
    )
    copies, born = lax.optimization_barrier((copies, born))
    total = jnp.sum(copies, axis=0)
    other = swap(total)
    ours, theirs = total[:2], other[:2]
    first_two = jnp.where(odd == 0, ours, theirs).reshape(2, 2, k, 128)
    third = jnp.where(odd == 0, theirs, ours)[:, :k]
    fourth = (total[2] + other[2]).reshape(2, k, 128)
    steps = jnp.concatenate([first_two, third[:, None], fourth[:, None]], axis=1)
    traces = steps.transpose(2, 1, 0, 3).reshape(k, ITERS, 256)
    return born.reshape(k, depth, nx, ny), traces


def solution(mesh):
    placed = (
        P(None, "tile", None),
        P(None, "tile", None),
        P(None, "tile", None),
        P(None, None, "tile", None),
        P("dir", None, "tile", None),
        P("dir", None, "tile", None),
        P("dir", "tile", None, None),
        P("tile", None),
        P("tile"),
        P(),
        P(),
        P(),
        P(),
        P(),
    )
    return jax.shard_map(
        local,
        mesh=mesh,
        in_specs=placed,
        out_specs=(P("dir", None, "tile", None), P("dir", None, None)),
        check_vma=False,
    )
```

```python
import functools

import jax
import jax.numpy as jnp
import numpy as np
from jax import lax
from jax.experimental import pallas as pl
from jax.experimental.pallas import tpu as pltpu
from jax.sharding import PartitionSpec as P

ITERS = 4
CAP = 2
F = 5

CENTRE = -14350.0
SECOND = (0.0, 8064.0, -1008.0, 128.0, -9.0)
FIRST = (0.0, 672.0, -168.0, 32.0, -3.0)

BF = jnp.bfloat16
F32 = jnp.float32
VM = pltpu.VMEM
SM = pltpu.SMEM


def vspec():
    return pl.BlockSpec(memory_space=VM)


def sspec():
    return pl.BlockSpec(memory_space=SM)


def params(mib=16):
    return pltpu.CompilerParams(vmem_limit_bytes=mib * 1024 * 1024)


def tap_matrix(ny):
    both = np.zeros((ny, 2 * ny), np.float32)
    for k in range(1, 5):
        for y in range(ny):
            for at, sign in ((y + k, 1.0), (y - k, -1.0)):
                if 0 <= at < ny:
                    both[at, y] = SECOND[k]
                    both[at, ny + y] = sign * FIRST[k]
    return np.concatenate([both, both], axis=0)


def pack_kernel(target, block, pieces, packed, count, label):
    directions, rows, zb, ny = pieces.shape
    tiles = packed.shape[0]

    def clear(t, c):
        count[t] = 0
        for a in range(CAP):
            label[t * CAP + a] = 0
        return c

    lax.fori_loop(0, tiles, clear, 0)

    def place(r, c):
        t = target[r]
        a = count[t]
        count[t] = a + 1
        label[t * CAP + a] = block[r] + 1
        for k in range(directions):
            at = pl.multiple_of((a * directions + k) * zb, zb)
            packed[t, pl.ds(at, zb), :] = pieces[k, r]
        return c

    lax.fori_loop(0, rows, place, 0)
    lane_at = lax.broadcasted_iota(jnp.int32, (16, ny), 1)

    def name(t, c):
        held = jnp.zeros((16, ny), jnp.int32)
        for a in range(CAP):
            held = jnp.where(lane_at == a, label[t * CAP + a], held)
        packed[t, CAP * directions * zb :, :] = held.astype(F32).astype(BF)
        return c

    lax.fori_loop(0, tiles, name, 0)


def pack(pieces, target, block, tiles):
    k, rows, zb, ny = pieces.shape
    return pl.pallas_call(
        pack_kernel,
        out_shape=jax.ShapeDtypeStruct((tiles, CAP * k * zb + 16, ny), pieces.dtype),
        in_specs=[sspec(), sspec(), vspec()],
        out_specs=vspec(),
        scratch_shapes=[SM((tiles,), jnp.int32), SM((tiles * CAP,), jnp.int32)],
        compiler_params=params(),
        name="pack",
    )(target, block, pieces)


def list_kernel(rz, rx, ry, where, rec):
    first, planes, depth = where[0], where[1], where[2]

    def look(i, n):
        x = rx[i] - first
        inside = (x >= 0) & (x < planes)
        beside = (x >= -4) & (x < planes + 4) & jnp.logical_not(inside)

        @pl.when(inside)
        def _():
            rec[0, n[0]] = x * depth + rz[i]
            rec[1, n[0]] = ry[i]
            rec[2, n[0]] = i

        @pl.when(beside)
        def _():
            rec[3, n[1]] = (x + 4) * depth + rz[i]
            rec[4, n[1]] = ry[i]
            rec[5, n[1]] = i

        return n[0] + inside.astype(jnp.int32), n[1] + beside.astype(jnp.int32)

    inner, outer = lax.fori_loop(0, rz.shape[0], look, (jnp.int32(0), jnp.int32(0)))
    rec[6, 0] = inner
    rec[6, 1] = outer


def list_receivers(rz, rx, ry, where):
    n = rz.shape[0]
    return pl.pallas_call(
        list_kernel,
        out_shape=jax.ShapeDtypeStruct((8, n), jnp.int32),
        in_specs=[sspec()] * 4,
        out_specs=sspec(),
        compiler_params=params(),
        name="receivers",
    )(rz, rx, ry, where)


def at_receivers(rec, read, into, gathered):
    for target in into:
        target[...] = jnp.zeros(target.shape, F32)
    for g in gathered:
        g[...] = jnp.zeros(g.shape, F32)
    lane = lax.broadcasted_iota(jnp.int32, gathered[0].shape, 1)

    def one(j, c):
        row, y, at = rec[0, j], rec[1, j], rec[2, j]
        read(row, gathered)
        to = at % 128
        for g, target in zip(gathered, into):
            moved = pltpu.roll(g[...], (to - y + 128) % 128, 1)
            target[at // 128] = target[at // 128] + jnp.where(lane == to, moved, 0.0)
        return c

    lax.fori_loop(0, rec[6, 0], one, 0)


def apply_own(cur, f, buf, ybuf, taps, coef, emit):
    nx, depth, ny = cur.shape[1:]
    for x in range(nx):
        u = cur[f, x]
        buf[4 + x, 8 : 8 + depth] = u
        top = u.astype(BF)
        rest = (u - top.astype(F32)).astype(BF)
        ybuf[x] = jnp.dot(
            jnp.concatenate([top, rest], axis=1), taps[...], preferred_element_type=F32
        )
    rows = 32

    def part(i, c):
        x, h = i // (depth // rows), i % (depth // rows)
        z0 = pl.multiple_of(h * rows, rows)
        at = 8 + z0

        def rd(px, dz):
            return buf[px, pl.ds(at + dz, rows), :]

        u = rd(4 + x, 0)
        y = ybuf[x, pl.ds(z0, rows), :]
        second = (3.0 * CENTRE) * u + y[:, :ny]
        gx = gz = None
        for k in range(1, 5):
            p, m = rd(4 + x + k, 0), rd(4 + x - k, 0)
            second = second + SECOND[k] * (p + m)
            g = FIRST[k] * (p - m)
            gx = g if gx is None else gx + g
            p, m = rd(4 + x, k), rd(4 + x, -k)
            second = second + SECOND[k] * (p + m)
            g = FIRST[k] * (p - m)
            gz = g if gz is None else gz + g

        def cf(which):
            return coef[which, x, pl.ds(z0, rows), :]

        value = cf(0) * second + cf(1) * gz + cf(2) * gx + cf(3) * y[:, ny:]
        emit(x, z0, rows, u, value)
        return c

    lax.fori_loop(0, nx * (depth // rows), part, 0)


def clear_edges(buf, depth):
    nx = buf.shape[0] - 8
    for x in range(4):
        buf[x] = jnp.zeros(buf.shape[1:], F32)
        buf[4 + nx + x] = jnp.zeros(buf.shape[1:], F32)
    zeros = jnp.zeros((8, buf.shape[2]), F32)
    for x in range(nx):
        buf[4 + x, 0:8] = zeros
        buf[4 + x, 8 + depth : 16 + depth] = zeros


def source_term(n, wav, src, x, z0, shape):
    z = lax.broadcasted_iota(jnp.int32, shape, 0) + z0
    y = lax.broadcasted_iota(jnp.int32, shape, 1)
    at = (z == src[0]) & (y == src[2])
    amount = jnp.where(x == src[1], wav[n], 0.0)
    return jnp.where(at, amount, 0.0)


def own_part(n, wav, src, cur, prev, coef, taps, part, acc, buf, ybuf):
    depth = cur.shape[2]
    clear_edges(buf, depth)
    for f in range(F):

        def emit(x, z0, rows, u, value, f=f):
            rs = pl.ds(z0, rows)
            new = 2.0 * u - prev[f, x, rs, :] + value
            if f == 0:
                acc[x, rs, :] = value
                new = new + source_term(n, wav, src, x, z0, u.shape)
            part[f, x, rs, :] = new

        apply_own(cur, f, buf, ybuf, taps, coef, emit)


def own_kernel(n, wav, src, cur, prev, coef, taps, part, acc, buf, ybuf):
    own_part(n, wav, src, cur, prev, coef, taps, part, acc, buf, ybuf)


def own_table_kernel(
    n, wav, src, *refs
):
    rec, cur, prev, coef, taps, perturb, part, acc, table, buf, ybuf, gathered, found = refs
    own_part(n, wav, src, cur, prev, coef, taps, part, acc, buf, ybuf)
    k, nx, depth, ny = perturb.shape

    def read(row, gs):
        x, z = row // depth, pl.ds(row % depth, 1)
        gs[0][0:1, :] = coef[0, x, z, :]
        gs[0][1:2, :] = coef[2, x, z, :]
        for j in range(k):
            gs[0][2 + j : 3 + j, :] = perturb[j, x, z, :]

    at_receivers(rec, read, [found], [gathered])
    left = found[...].reshape(16, 128)
    for term in range(3):
        rounded = left.astype(BF)
        table[16 * term : 16 * term + 16, :] = rounded
        left = left - rounded.astype(F32)
    table[48:64, :] = jnp.zeros((16, 128), BF)


def share_kernel(*refs):
    rec, cur, prev, coef, perturb, table, traces = refs[:7]
    gathered, found = refs[7:13], refs[13:19]
    k, nx, depth, ny = perturb.shape
    lane = lax.broadcasted_iota(jnp.int32, (8, 128), 1)
    for ref in gathered + found:
        ref[...] = jnp.zeros(ref.shape, F32)

    g2, g1 = gathered[:2]
    t2, t1 = found[:2]

    def beside(i, c):
        row, y, at = rec[3, i], rec[4, i], rec[5, i]
        x, z = row // depth - 4, pl.ds(row % depth, 1)
        near = jnp.where(x < 0, 0, nx - 4)
        weights = []
        for q in range(4):
            d = near + q - x
            away = jnp.abs(d)
            c2 = c1 = jnp.float32(0.0)
            for t in range(1, 5):
                c2 = jnp.where(away == t, jnp.float32(SECOND[t]), c2)
                c1 = jnp.where(away == t, jnp.float32(FIRST[t]), c1)
            weights.append((c2, jnp.where(d < 0, -c1, c1)))
        for f in range(F):
            second = first = jnp.zeros((1, ny), F32)
            for q in range(4):
                u = cur[f, near + q, z, :]
                second = second + weights[q][0] * u
                first = first + weights[q][1] * u
            g2[f : f + 1, :] = second
            g1[f : f + 1, :] = first
        to = at % 128
        shift = (to - y + 128) % 128
        here = lane == to
        h = at // 128
        t2[h] = t2[h] + jnp.where(here, pltpu.roll(g2[...], shift, 1), 0.0)
        t1[h] = t1[h] + jnp.where(here, pltpu.roll(g1[...], shift, 1), 0.0)
        return c

    lax.fori_loop(0, rec[6, 1], beside, 0)
    for h in range(2):
        const = table[8 * h : 8 * h + 8, :]
        reach = const[0:1] * t2[h] + const[1:2] * t1[h]
        for j in range(k):
            traces[h * k + j : h * k + j + 1, :] = (
                reach[1 + j : 2 + j] + const[2 + j : 3 + j] * reach[0:1]
            )

    for ref in found:
        ref[...] = jnp.zeros(ref.shape, F32)
    gs, gz, gx, gu, gp, gc = gathered
    fs, fz, fx, fy, fu, fc = found

    def inside(at, size, weight):
        return jnp.where((at >= 0) & (at < size), jnp.float32(weight), jnp.float32(0.0))

    def own(i, c):
        row, y, at = rec[0, i], rec[1, i], rec[2, i]
        x, z = row // depth, row % depth
        here_z = pl.ds(z, 1)
        reach = []
        for d in (1, 2, 3, 4, -1, -2, -3, -4):
            t = abs(d)
            sign = 1.0 if d > 0 else -1.0
            px, pz = jnp.clip(x + d, 0, nx - 1), jnp.clip(z + d, 0, depth - 1)
            reach.append(
                (
                    px,
                    inside(x + d, nx, SECOND[t]),
                    inside(x + d, nx, sign * FIRST[t]),
                    pl.ds(pz, 1),
                    inside(z + d, depth, SECOND[t]),
                    inside(z + d, depth, sign * FIRST[t]),
                )
            )
        for f in range(F):
            u = cur[f, x, here_z, :]
            second = (3.0 * CENTRE) * u
            along_x = along_z = jnp.zeros((1, ny), F32)
            for px, x2, x1, pz, z2, z1 in reach:
                v = cur[f, px, here_z, :]
                w = cur[f, x, pz, :]
                second = second + x2 * v + z2 * w
                along_x = along_x + x1 * v
                along_z = along_z + z1 * w
            gs[f : f + 1, :] = second
            gz[f : f + 1, :] = along_z
            gx[f : f + 1, :] = along_x
            gu[f : f + 1, :] = u
            gp[f : f + 1, :] = 2.0 * u - prev[f, x, here_z, :]
        for a in range(4):
            gc[a : a + 1, :] = coef[a, x, here_z, :]
        for j in range(k):
            gc[4 + j : 5 + j, :] = perturb[j, x, here_z, :]
        to = at % 128
        shift = to - y + 256
        here = lane == to
        h = at // 128

        def moved(ref, by=0):
            return pltpu.roll(ref[...], (shift - by) % 128, 1)

        second, along_y = moved(gs), jnp.zeros((8, 128), F32)
        for d in (1, 2, 3, 4, -1, -2, -3, -4):
            t = abs(d)
            v = moved(gu, d)
            second = second + inside(y + d, ny, SECOND[t]) * v
            along_y = along_y + inside(y + d, ny, FIRST[t] if d > 0 else -FIRST[t]) * v
        for ref, value in (
            (fs, second),
            (fz, moved(gz)),
            (fx, moved(gx)),
            (fy, along_y),
            (fu, moved(gp)),
            (fc, moved(gc)),
        ):
            ref[h] = ref[h] + jnp.where(here, value, 0.0)
        return c

    lax.fori_loop(0, rec[6, 0], own, 0)
    for h in range(2):
        con = fc[h]
        value = con[0:1] * fs[h] + con[1:2] * fz[h] + con[2:3] * fx[h] + con[3:4] * fy[h]
        base = fu[h] + value
        for j in range(k):
            at = slice(h * k + j, h * k + j + 1)
            traces[at, :] = (
                traces[at, :] + base[1 + j : 2 + j] + con[4 + j : 5 + j] * value[0:1]
            )


def near_planes(msg, f, first, rs):
    if first and f > 0:
        base = 5 + 4 * (f - 1)
        return [msg[base + p, rs, :].astype(F32) for p in range(4)]
    base = 5 * f
    near = msg[base, rs, :].astype(F32) + msg[base + 1, rs, :].astype(F32)
    return [near] + [msg[base + 1 + p, rs, :].astype(F32) for p in range(1, 4)]


def send_plane(msg, f, p, rs, new):
    top = new.astype(BF)
    if p == 0:
        msg[5 * f, rs, :] = top
        msg[5 * f + 1, rs, :] = (new - top.astype(F32)).astype(BF)
    else:
        msg[5 * f + 1 + p, rs, :] = top


def finish_part(n, part, acc_own, low_in, high_in, coef, perturb, acc, nxt, low, high, out):
    nx, depth, ny = part.shape[1:]
    rows = 16
    last = n == ITERS - 1
    for f in range(F):

        def piece(i, c, f=f):
            z0 = pl.multiple_of(i * rows, rows)
            rs = pl.ds(z0, rows)
            below = near_planes(low_in, f, n == 0, rs)
            above = near_planes(high_in, f, n == 0, rs)
            for x in range(nx):
                lower = x < 4
                planes, d, sign = (below, x, -1.0) if lower else (above, nx - 1 - x, 1.0)
                second = first = None
                for j in range(4 - d):
                    t = d + 1 + j
                    s, g = SECOND[t] * planes[j], (sign * FIRST[t]) * planes[j]
                    second = s if second is None else second + s
                    first = g if first is None else first + g
                reach = coef[0, x, rs, :] * second + coef[2, x, rs, :] * first
                if f == 0:
                    acc[x, rs, :] = acc_own[x, rs, :] + reach
                    if last:
                        continue
                    new = part[f, x, rs, :] + reach
                else:
                    new = part[f, x, rs, :] + reach + perturb[f - 1, x, rs, :] * acc[x, rs, :]
                if last:
                    out[f - 1, pl.ds(z0 * nx + x, rows, stride=nx), :] = new
                else:
                    nxt[f, x, rs, :] = new
                    send_plane(low if lower else high, f, d, rs, new)
            return c

        lax.fori_loop(0, depth // rows, piece, 0)


def by_parity(odd, run):
    @pl.when(odd == 0)
    def _():
        run(True)

    @pl.when(odd == 1)
    def _():
        run(False)


def sample_new(n, rec, nxt, traces, gathered, depth, k):
    offset = (n % 2) * k

    def read(row, gs):
        for j in range(k):
            gs[0][offset + j : offset + j + 1, :] = nxt[
                j + 1, row // depth, pl.ds(row % depth, 1), :
            ]

    at_receivers(rec, read, [traces], [gathered])


def gather_kernel(*refs):
    src, rec = refs[:2]
    far = refs[2:8]
    nxt, perturb, away, beside, traces = refs[8:13]
    near = refs[13:19]
    acc, gathered, names, labels, arrived, landed = refs[19:]
    loads = [pltpu.make_async_copy(a, b, landed.at[i]) for i, (a, b) in enumerate(zip(far, near))]
    for load in reversed(loads):
        load.start()
    part, acc_own, away_in, beside_in, coef, incoming = near
    k, nx, depth, ny = perturb.shape
    loads[5].wait()
    zb = (incoming.shape[1] - 16) // (CAP * k)
    for t in range(incoming.shape[0]):
        names[t : t + 1, :] = (
            incoming[t, CAP * k * zb : CAP * k * zb + 16, :].astype(F32)[0:1].astype(jnp.int32)
        )
    copy = pltpu.make_async_copy(names, labels, arrived)
    copy.start()
    perturb[...] = jnp.zeros(perturb.shape, F32)
    copy.wait()

    def add(s, c):
        t, a = s // CAP, s % CAP
        label = labels[t, a]

        @pl.when(label > 0)
        def _():
            b = label - 1
            x = b % nx
            z0 = pl.multiple_of((b // nx) * zb, zb)
            for j in range(k):
                at = pl.multiple_of((a * k + j) * zb, zb)
                perturb[j, x, pl.ds(z0, zb), :] = perturb[j, x, pl.ds(z0, zb), :] + incoming[
                    t, pl.ds(at, zb), :
                ].astype(F32)

        return c

    lax.fori_loop(0, incoming.shape[0] * CAP, add, 0, unroll=8)
    for load in loads[:5]:
        load.wait()

    def run(even):
        low_in, high_in = (away_in, beside_in) if even else (beside_in, away_in)
        low, high = (away, beside) if even else (beside, away)
        finish_part(0, part, acc_own, low_in, high_in, coef, perturb, acc, nxt, low, high, None)

    by_parity(src[3], run)
    sample_new(0, rec, nxt, traces, gathered, depth, k)


def finish_kernel(n, src, *refs):
    last = n == ITERS - 1
    rec = None
    if not last:
        rec, refs = refs[0], refs[1:]
    part, acc_own, away_in, beside_in, coef, perturb = refs[:6]
    rest = refs[6:]
    k, nx, depth, ny = perturb.shape
    out = nxt = away = beside = None
    if last:
        out, acc = rest
    elif n == 1:
        table, nxt, away, beside, traces, acc, gathered = rest
        away[5 * F] = table[...]
        beside[5 * F] = table[...]
    else:
        early, nxt, away, beside, traces, found, acc, gathered = rest
        both = jnp.zeros((16, 128), F32)
        for msg in (away_in, beside_in):
            for term in range(3):
                both = both + msg[5 * F, 16 * term : 16 * term + 16, :].astype(F32)
        found[...] = both

    def run(even):
        low_in, high_in = (away_in, beside_in) if even else (beside_in, away_in)
        low, high = (away, beside) if even else (beside, away)
        finish_part(n, part, acc_own, low_in, high_in, coef, perturb, acc, nxt, low, high, out)

    by_parity(src[3], run)
    if last:
        return
    sample_new(n, rec, nxt, traces, gathered, depth, k)
    if n == 2:
        left = jnp.concatenate([early[...].reshape(16, 128), traces[...].reshape(16, 128)])
        for term in range(4):
            rounded = left.astype(BF) if term < 3 else jnp.zeros((32, 128), BF)
            beside[5 * F + term // 2, 32 * (term % 2) : 32 * (term % 2) + 32, :] = rounded
            left = left - rounded.astype(F32)


def message_kernel(src, beside, two, third, mine, out):
    own = jnp.concatenate([two[...].reshape(16, 128), third[...].reshape(16, 128)])
    theirs = beside[5 * F, 0:32, :].astype(F32) + beside[5 * F, 32:64, :].astype(F32)
    both = own + (theirs + beside[5 * F + 1, 0:32, :].astype(F32))
    half = jnp.where(src[3] == 0, both[0:16], both[16:32])
    message = jnp.concatenate([half, mine[...]]).reshape(3, 8, 128)
    for i in range(out.shape[0]):
        out[i] = message


def cost(flops, moved):
    return pl.CostEstimate(flops=flops, bytes_accessed=moved, transcendentals=0)


def exchange(away, beside):
    count = lax.axis_size("tile")
    pairs = [(i, i + 1) for i in range(1, count - 1, 2)]
    there = lax.ppermute(away, "tile", pairs + [(b, a) for a, b in pairs])
    return there, swap(beside)


def swap(value):
    count = lax.axis_size("tile")
    return lax.ppermute(value, "tile", [(i, i ^ 1) for i in range(count)])


def two_terms(plane):
    top = plane.astype(BF)
    return [top, (plane - lax.reduce_precision(plane, 8, 7)).astype(BF)]


def local(
    background_prev,
    background_now,
    stiffness,
    drift_terms,
    born_prev,
    born_now,
    pieces,
    piece_target,
    piece_block,
    wavelet,
    source_cell,
    receiver_z,
    receiver_x,
    receiver_y,
):
    tiles = lax.axis_size("tile")
    place = lax.axis_index("tile")
    k = born_now.shape[0]
    depth, nx, ny = background_now.shape
    zb = pieces.shape[2]

    odd = place % 2
    packed = pack(pieces, piece_target[:, 0], piece_block, tiles)
    incoming = lax.all_to_all(packed, "tile", 0, 0, tiled=True)

    def face(planes):
        near = two_terms(background_now[:, planes[0], :])
        rows = near + [background_now[:, p, :].astype(BF) for p in planes[1:]]
        born = jnp.stack([born_now[:, :, p, :] for p in planes], axis=1)
        return jnp.concatenate([jnp.stack(rows), born.reshape(k * 4, depth, ny)])

    low, high = face((0, 1, 2, 3)), face((7, 6, 5, 4))
    low_in, high_in = exchange(jnp.where(odd == 0, low, high), jnp.where(odd == 0, high, low))

    where = jnp.stack([place * nx, jnp.int32(nx), jnp.int32(depth)]).astype(jnp.int32)
    rec = list_receivers(receiver_z, receiver_x, receiver_y, where)
    src = jnp.stack([source_cell[0], source_cell[1] - place * nx, source_cell[2], odd])

    def planes_first(background, born):
        return jnp.concatenate(
            [
                background.transpose(1, 0, 2)[None],
                born.astype(F32).transpose(0, 2, 1, 3),
            ]
        )

    cur = planes_first(background_now, born_now)
    prev = planes_first(background_prev, born_prev)
    coef = jnp.concatenate(
        [
            (stiffness.astype(F32) * (1.0 / 5040.0))[None],
            drift_terms.astype(F32) * (1.0 / 840.0),
        ]
    ).transpose(0, 2, 1, 3)
    taps = jnp.asarray(tap_matrix(ny)).astype(BF)

    state = jax.ShapeDtypeStruct((F, nx, depth, ny), F32)
    field = jax.ShapeDtypeStruct((nx, depth, ny), F32)
    faces = jax.ShapeDtypeStruct((5 * F, depth, ny), BF)
    wider = jax.ShapeDtypeStruct((5 * F + 1, depth, ny), BF)
    widest = jax.ShapeDtypeStruct((5 * F + 2, depth, ny), BF)
    traced = jax.ShapeDtypeStruct((2, 8, 128), F32)
    small = VM((8, 128), F32)
    pair = VM((2, 8, 128), F32)
    work = [VM((nx + 8, depth + 16, ny), F32), VM((nx, depth, 2 * ny), F32)]
    cells = F * nx * depth * ny

    def call(kernel, name, out_shape, scratch, scalars, arrays, flops, spec=vspec(), mib=16):
        return pl.pallas_call(
            kernel,
            out_shape=out_shape,
            in_specs=[sspec()] * len(scalars) + [spec] * len(arrays),
            out_specs=tuple(vspec() for _ in out_shape),
            scratch_shapes=scratch,
            compiler_params=params(mib),
            cost_estimate=cost(flops * cells, 16 * cells),
            name=name,
        )(*scalars, *arrays)

    records = []
    perturb = table = found = None
    for n in range(ITERS):
        name = "own%d" % (n + 1)
        start = (wavelet, src)
        arrays = (cur, prev, coef, taps)
        if n == 1:
            part, acc, table = call(
                functools.partial(own_table_kernel, n),
                name,
                (state, field, jax.ShapeDtypeStruct((64, 128), BF)),
                work + [small, pair],
                start + (rec,),
                arrays + (perturb,),
                80,
            )
        elif n == ITERS - 1:
            (mine,) = call(
                share_kernel,
                "share",
                (jax.ShapeDtypeStruct((8, 128), F32),),
                [small] * 6 + [pair] * 6,
                (rec,),
                (cur, prev, coef, perturb, found),
                20,
            )
            part, acc = call(
                functools.partial(own_kernel, n), name, (state, field), work, start, arrays, 80000
            )
        else:
            part, acc = call(
                functools.partial(own_kernel, n),
                name,
                (state, field),
                work,
                start,
                arrays,
                80,
            )
        arrays = (part, acc, low_in, high_in, coef)
        name = "finish%d" % (n + 1)
        keep = VM((nx, depth, ny), F32)
        if n == 0:
            nxt, perturb, low, high, traces = call(
                gather_kernel,
                name,
                (state, jax.ShapeDtypeStruct((k, nx, depth, ny), F32), faces, faces, traced),
                [VM(a.shape, a.dtype) for a in arrays + (incoming,)]
                + [
                    keep,
                    small,
                    VM((tiles, 128), jnp.int32),
                    SM((tiles, 128), jnp.int32),
                    pltpu.SemaphoreType.DMA,
                    pltpu.SemaphoreType.DMA((6,)),
                ],
                (src, rec),
                arrays + (incoming,),
                20,
                pl.BlockSpec(memory_space=pltpu.HBM),
                58,
            )
        elif n == ITERS - 1:
            (born,) = call(
                functools.partial(finish_kernel, n),
                name,
                (jax.ShapeDtypeStruct((k, depth * nx, ny), F32),),
                [keep],
                (src,),
                arrays + (perturb,),
                20,
            )
            break
        else:
            face_type = wider if n == 1 else faces
            inner_type = wider if n == 1 else widest
            if n == 2:
                two = records[0] + records[1]
            extra = table if n == 1 else two
            more = () if n == 1 else (jax.ShapeDtypeStruct((16, 128), F32),)
            nxt, low, high, traces, *more = call(
                functools.partial(finish_kernel, n),
                name,
                (state, face_type, inner_type, traced) + more,
                [keep, small],
                (src, rec),
                arrays + (perturb, extra),
                20,
            )
            if n == 2:
                (found,) = more
        records.append(traces)
        low_in, high_in = exchange(low, high)
        prev, cur = cur, nxt

    (sent,) = call(
        message_kernel,
        "message",
        (jax.ShapeDtypeStruct((tiles // 2, 3, 8, 128), F32),),
        [],
        (src,),
        (high_in, two, records[2], mine),
        1,
    )
    groups = [list(range(c, tiles, 2)) for c in range(2)]
    copies = lax.all_to_all(
        sent,
        "tile",
        0,
        0,
        axis_index_groups=groups,
        tiled=True,
    )
    copies, born = lax.optimization_barrier((copies, born))
    total = jnp.sum(copies, axis=0)
    other = swap(total)
    ours, theirs = total[:2], other[:2]
    first_two = jnp.where(odd == 0, ours, theirs).reshape(2, 2, k, 128)
    third = jnp.where(odd == 0, theirs, ours)[:, :k]
    fourth = (total[2] + other[2]).reshape(2, k, 128)
    steps = jnp.concatenate([first_two, third[:, None], fourth[:, None]], axis=1)
    traces = steps.transpose(2, 1, 0, 3).reshape(k, ITERS, 256)
    return born.reshape(k, depth, nx, ny), traces


def solution(mesh):
    placed = (
        P(None, "tile", None),
        P(None, "tile", None),
        P(None, "tile", None),
        P(None, None, "tile", None),
        P("dir", None, "tile", None),
        P("dir", None, "tile", None),
        P("dir", "tile", None, None),
        P("tile", None),
        P("tile"),
        P(),
        P(),
        P(),
        P(),
        P(),
    )
    return jax.shard_map(
        local,
        mesh=mesh,
        in_specs=placed,
        out_specs=(P("dir", None, "tile", None), P("dir", None, None)),
        check_vma=False,
    )
```
